512 devices in a mesh: dp: 64 (over y_lo, x, z), space: 8 (over y_hi, core).
Axes of the slice: x: 4, y: 8 (y_hi: 4, y_lo: 2; y = y_hi * 2 + y_lo), z: 8, core: 2. Of those that a mesh axis runs over, the one named last changes fastest.
Arguments:
- field_in: bfloat16 [1, 512, 512, 128], P(None, 'space', 'dp'), may hold values from -6 to 6
- pre_act: bfloat16 [1, 512, 512, 128], P(None, 'space', 'dp'), may hold values from -8 to 8
- cotangent: bfloat16 [1, 512, 512, 128], P(None, 'space', 'dp'), may hold values from -6 to 6
- spec_weight: bfloat16 [64, 64, 2, 128, 128], P('dp', 'space'), may hold values from -0.25 to 0.25
- local_weight: bfloat16 [128, 128], replicated, may hold values from -0.5 to 0.5
Outputs:
- grad_input: bfloat16 [1, 512, 512, 128], P(None, 'space', 'dp')
- grad_spectral: bfloat16 [64, 64, 2, 128, 128], P('dp', 'space')
- grad_local: float32 [128, 128], replicated
- grad_bias: float32 [128], replicated
The draws below stay inside these ranges and needn't reach their ends.
All inputs are finite; a program needn't handle non-finite values.
Results may differ from the reference program's by a relative error of at most 0.0075.
The reference program's roundings to bfloat16 on the way (of `delta_field`, `y_table`, `x_table`, `along_y`, `mode_back`, `along_x` and `spectral_part`) count: a program that leaves them out, or rounds other values in their place, can miss the bound.
Values may be sent and summed in bfloat16 or wider, within the bound.
A program may use at most 64 MiB of HBM per device.

```python
import math
import jax
import jax.numpy as jnp
from jax import lax

C = 128
KX = 64
KY = 64
NX = 512
NY = 512
BATCH = 1


def shard_levels(stream_key, extent, cuts, smallest, high):
    gain, own = 1.0, jax.random.fold_in(stream_key, 6)
    for dim, shards_of in cuts:
        draws = jnp.exp(jax.random.uniform(jax.random.fold_in(own, dim), (shards_of,), jnp.float32, smallest / len(cuts), high / len(cuts)))
        gain = gain * jnp.repeat(draws, extent[dim] // shards_of).reshape([-1 if axis == dim else 1 for axis in range(len(extent))])
    return gain


def noise(own_key, shape, spread, bound, pieces=(), kind=jnp.bfloat16):
    loudness = shard_levels(own_key, shape, pieces, -0.22, 0.18) if pieces else 1.0
    drawn = jax.random.normal(own_key, shape, jnp.float32) * spread * loudness
    return jnp.minimum(jnp.maximum(drawn, -bound), bound).astype(kind)


def setup_inputs(seed: int = 0) -> dict:
    splits = jax.random.split(jax.random.key(seed), 6)
    return {
        "field_in": noise(splits[0], (BATCH, NX, NY, C), 1.0, 6.0, ((1, 8), (2, 64))),
        "pre_act": noise(splits[1], (BATCH, NX, NY, C), 1.5, 8.0, ((1, 8), (2, 64))),
        "cotangent": noise(splits[2], (BATCH, NX, NY, C), 1.0, 6.0, ((1, 8), (2, 64))),
        "spec_weight": noise(splits[3], (KX, KY, 2, C, C), (4 * C) ** -0.5, 0.25, ((0, 64), (1, 8))),
        "local_weight": noise(splits[4], (C, C), C ** -0.5, 0.5),
    }


highest = lax.Precision.HIGHEST
root_two_pi = 0.7978845608028654
cubic_coef = 0.044715

def gelu_slope(values):
    tangent = jnp.tanh(root_two_pi * (values + cubic_coef * values * values * values))
    return 0.5 * (1.0 + tangent) + 0.5 * values * (1.0 - tangent * tangent) * root_two_pi * (1.0 + 3.0 * cubic_coef * values * values)

def y_basis(grid_cols, ky_count):
    positions = jnp.arange(grid_cols, dtype=jnp.int32)
    frequency = jnp.arange(ky_count, dtype=jnp.int32)
    phases = positions[:, None] * frequency[None, :] % grid_cols
    angles = phases.astype(jnp.float32) * (2.0 * math.pi / grid_cols)
    basis_table = jnp.stack([jnp.cos(angles), -jnp.sin(angles)], axis=2).reshape(grid_cols, 2 * ky_count)
    return basis_table.astype(jnp.bfloat16)

def x_basis(grid_rows, kx_count):
    positions = jnp.arange(grid_rows, dtype=jnp.int32)
    mode_index = jnp.arange(kx_count, dtype=jnp.int32)
    frequency = jnp.where(mode_index < kx_count // 2, mode_index, mode_index - kx_count)
    phases = frequency[:, None] * positions[None, :] % grid_rows
    angles = phases.astype(jnp.float32) * (2.0 * math.pi / grid_rows)
    cosine = jnp.cos(angles)
    sine = jnp.sin(angles)
    upper_rows = jnp.stack([cosine, sine], axis=1)
    lower_rows = jnp.stack([-sine, cosine], axis=1)
    return jnp.stack([upper_rows, lower_rows], axis=0).astype(jnp.bfloat16)

def rounded(values):
    return lax.optimization_barrier(values.astype(jnp.bfloat16)).astype(jnp.float32)

def reference(field_in, pre_act, cotangent, spec_weight, local_weight):
    y_table = y_basis(NY, KY).astype(jnp.float32)
    x_table = x_basis(NX, KX).astype(jnp.float32)
    local_float = local_weight.astype(jnp.float32)

    def forward_sample(inputs):
        sample, pre_sample, cot_sample = inputs
        delta_field = (cot_sample.astype(jnp.float32) * gelu_slope(pre_sample.astype(jnp.float32))).astype(jnp.bfloat16)
        stacked = jnp.stack([sample, delta_field]).astype(jnp.float32)
        along_y = rounded(jnp.einsum('fxyc,yr->fxrc', stacked, y_table, precision=highest))
        along_y = along_y.reshape(2, NX, KY, 2, C)
        spectra = jnp.einsum('qjpx,fxkpc->fjkqc', x_table, along_y, precision=highest).astype(jnp.bfloat16)
        local_term = jnp.einsum('xyc,xyo->co', sample.astype(jnp.float32), delta_field.astype(jnp.float32), precision=highest)
        bias_term = lax.optimization_barrier(jnp.sum(delta_field.astype(jnp.float32), axis=(0, 1)))
        return (spectra, delta_field, local_term, bias_term)
    spectra, deltas, local_terms, bias_terms = lax.map(forward_sample, (field_in, pre_act, cotangent))
    ky_scale = jnp.where(jnp.arange(KY, dtype=jnp.int32) == 0, 1.0, 2.0).astype(jnp.float32) / (NX * NY)
    per_mode = jnp.moveaxis(spectra, 2, 0)

    def mode_column(inputs):
        column, weights = inputs
        input_part = column[:, 0].astype(jnp.float32)
        delta_part = column[:, 1].astype(jnp.float32)
        products = jnp.einsum('bkqc,bkpo->kqpco', input_part, delta_part, precision=highest)
        grad_real = products[:, 0, 0] + products[:, 1, 1]
        grad_imag = products[:, 0, 1] - products[:, 1, 0]
        grad_mode = (jnp.stack([grad_real, grad_imag], axis=1) * (ky_scale / BATCH)[:, None, None, None]).astype(jnp.bfloat16)
        adjoint = jnp.einsum('bkpo,kqco->bkpqc', delta_part, weights.astype(jnp.float32), precision=highest)
        back_real = adjoint[:, :, 0, 0] + adjoint[:, :, 1, 1]
        back_imag = adjoint[:, :, 1, 0] - adjoint[:, :, 0, 1]
        mode_grad = (jnp.stack([back_real, back_imag], axis=2) * ky_scale[None, :, None, None]).astype(jnp.bfloat16)
        return (grad_mode, mode_grad)
    grad_spectral, mode_back = lax.map(mode_column, (per_mode, spec_weight))
    back_per_sample = jnp.moveaxis(mode_back, 1, 0)

    def input_grad(inputs):
        modes, delta_field = inputs
        along_x = rounded(jnp.einsum('qjpx,jkqc->xkpc', x_table, modes.astype(jnp.float32), precision=highest))
        along_x = along_x.reshape(NX, 2 * KY, C)
        spectral_part = rounded(jnp.einsum('xrc,yr->xyc', along_x, y_table, precision=highest))
        local_part = jnp.einsum('xyo,co->xyc', delta_field.astype(jnp.float32), local_float, precision=highest)
        return (spectral_part + local_part).astype(jnp.bfloat16)
    grad_input = lax.map(input_grad, (back_per_sample, deltas))
    grad_local = lax.optimization_barrier(jnp.sum(local_terms, axis=0)) / BATCH
    grad_bias = lax.optimization_barrier(jnp.sum(bias_terms, axis=0)) / BATCH
    return (grad_input, grad_spectral, grad_local, grad_bias)
```

```python
import math

import jax
import jax.numpy as jnp
import numpy as np
from jax import lax
from jax.experimental import pallas as pl
from jax.experimental.pallas import tpu as pltpu
from jax.sharding import PartitionSpec as P

root_two_pi = 0.7978845608028654
cubic_coef = 0.044715

N = 8
C = 128
GRID = 512
MODES = 64
f32 = jnp.float32
bf16 = jnp.bfloat16

FIELDS, SPEC_Z, SPEC_YX, PARTIAL, BACK, BACK_YX, BACK_Z, ROWS, SUM_SPACE, SUM_Z, SUM_YX, SUM_BACK = range(12)


def gelu_slope(values):
    tangent = jnp.tanh(root_two_pi * (values + cubic_coef * values * values * values))
    return 0.5 * (1.0 + tangent) + 0.5 * values * (1.0 - tangent * tangent) * root_two_pi * (
        1.0 + 3.0 * cubic_coef * values * values
    )


def trig(phases):
    angles = (phases % GRID).astype(np.float32) * np.float32(2.0 * math.pi / GRID)
    return np.cos(angles), np.sin(angles)


def tables():
    j = (np.arange(N)[None, :] * N + np.arange(N)[:, None]).reshape(MODES)
    frequency = np.where(j < MODES // 2, j, j - MODES)
    c, s = trig(frequency[:, None] * np.arange(GRID)[None, :])
    x_table = np.stack([c, s], axis=1).reshape(2 * MODES, GRID)
    y = np.arange(MODES)[None, :] * N + np.arange(N)[:, None]
    c, s = trig(np.arange(MODES)[None, :, None] * y[:, None, :])
    y_table = np.stack([np.stack([c, -s], axis=3), np.stack([-s, -c], axis=3)], axis=2)
    y_table = y_table.reshape(N, 2 * MODES, 2 * MODES)
    y_tables = np.stack([y_table, np.swapaxes(y_table, 1, 2)], axis=1)
    order = np.arange(2 * MODES).reshape(N, N, 2).swapaxes(0, 1).reshape(-1)
    swap = np.eye(2 * MODES)[order]
    return [t.astype(bf16) for t in (x_table, np.ascontiguousarray(x_table.T), y_tables, swap)]


def dot(a, b):
    return jnp.dot(a, b, preferred_element_type=f32)


def dot_nt(a, b):
    return lax.dot_general(a, b, (((1,), (1,)), ((), ())), preferred_element_type=f32)


def kernel(
    field_hbm, pre_hbm, cot_hbm, weight_hbm, lw_hbm, xt_hbm, xtt_hbm, yt_hbm, swap_hbm,
    out_grad, out_spec, out_local, out_bias,
    field_v, pre_v, cot_v, weight, lw, xt, xtt, yt, swap,
    rows_f, rows_d, send1, recv1, local_part,
    send2, recv2, send3, recv3, send4, recv4, send5, recv5, send6, recv6, send7, recv7, send8, recv8,
    sum_send, sum_recv, sumz_send, sumz_recv, sumy_send, sumy_recv, sumb_send, sumb_recv,
    grads, in_sem, out_sem, send_sem, recv_sem,
):
    sp = lax.axis_index("space")
    dp = lax.axis_index("dp")
    yx = dp // N
    z = dp - yx * N

    def peer(axis, o):
        if axis == "space":
            other = lax.rem(sp + o, N)
            return other, sp, {"dp": dp, "space": other}
        if axis == "z":
            other = lax.rem(z + o, N)
            return other, z, {"dp": yx * N + other, "space": sp}
        other = lax.rem(yx + o, N)
        return other, yx, {"dp": other * N + z, "space": sp}

    barrier = pltpu.get_barrier_semaphore()
    for o in range(1, N):
        for axis in ("space", "z", "yx"):
            pl.semaphore_signal(barrier, inc=1, device_id=peer(axis, o)[2])

    loads = []
    for i, (src, dst) in enumerate((
        (pre_hbm.at[0], pre_v), (cot_hbm.at[0], cot_v), (field_hbm.at[0], field_v), (xt_hbm, xt),
        (lw_hbm, lw), (swap_hbm, swap), (yt_hbm.at[sp], yt), (weight_hbm, weight), (xtt_hbm, xtt),
    )):
        loads.append(pltpu.make_async_copy(src, dst, in_sem.at[i]))
        loads[-1].start()

    started = []

    def send(hop, axis, o, src, dst, each):
        other, me, device = peer(axis, o)
        copy = pltpu.make_async_remote_copy(
            src_ref=src.at[other] if each else src,
            dst_ref=dst.at[me],
            send_sem=send_sem.at[hop, o],
            recv_sem=recv_sem.at[hop, me],
            device_id=device,
        )
        copy.start()
        started.append(copy)

    def send_all(hop, axis, src, dst, each=True):
        for o in range(1, N):
            send(hop, axis, o, src, dst, each)
        me = peer(axis, 0)[1]
        dst[me] = src[me] if each else src[...]

    def wait_all(hop, axis, dst):
        for o in range(1, N):
            other, me, device = peer(axis, o)
            pltpu.make_async_remote_copy(
                src_ref=dst.at[other],
                dst_ref=dst.at[other],
                send_sem=send_sem.at[hop, o],
                recv_sem=recv_sem.at[hop, other],
                device_id=device,
            ).wait_recv()

    def total(ref):
        acc = ref[0]
        for i in range(1, N):
            acc = acc + ref[i]
        return acc

    for i in range(3):
        loads[i].wait()
    delta = (cot_v[...].astype(f32) * gelu_slope(pre_v[...].astype(f32))).astype(bf16).astype(f32)
    rows_d[...] = delta.reshape(GRID, C)
    rows_f[...] = field_v[...].astype(f32).reshape(GRID, C)
    bias_part = jnp.sum(delta, axis=0)
    for t in range(N):
        send1[t, :, 0:C] = rows_f[pl.ds(t, MODES, stride=N), :].astype(bf16)
        send1[t, :, C:] = rows_d[pl.ds(t, MODES, stride=N), :].astype(bf16)
    pl.semaphore_wait(barrier, 3 * (N - 1))
    send_all(FIELDS, "space", send1, recv1)

    both = send1[...].reshape(GRID, 2 * C)
    local = lax.dot_general(
        both[:, 0:C], both[:, C:], (((0,), (0,)), ((), ())), preferred_element_type=f32
    )
    for t in range(N):
        sum_send[t, 0:16, :] = local[16 * t : 16 * t + 16, :]
        sum_send[t, 16:24, :] = bias_part
    send_all(SUM_SPACE, "space", sum_send, sum_recv)
    for i in range(3, 9):
        loads[i].wait()
    local_part[...] = dot_nt(both[:, C:], lw[...]).reshape(N, MODES, C)

    wait_all(FIELDS, "space", recv1)
    send2[...] = dot(xt[...], recv1[...].reshape(GRID, 2 * C)).astype(bf16).reshape(N, 16, 2 * C)
    send_all(SPEC_Z, "z", send2, recv2)

    wait_all(SUM_SPACE, "space", sum_recv)
    sumz_send[...] = total(sum_recv)
    send_all(SUM_Z, "z", sumz_send, sumz_recv, each=False)

    wait_all(SPEC_Z, "z", recv2)
    send3[...] = dot(swap[...], recv2[...].reshape(2 * MODES, 2 * C)).astype(bf16).reshape(N, 16, 2 * C)
    send_all(SPEC_YX, "yx", send3, recv3)

    wait_all(SUM_Z, "z", sumz_recv)
    sumy_send[...] = total(sumz_recv)
    send_all(SUM_YX, "yx", sumy_send, sumy_recv, each=False)

    wait_all(SPEC_YX, "yx", recv3)
    send4[...] = dot(yt[0], recv3[...].reshape(2 * MODES, 2 * C)).reshape(N, 16, 2 * C)
    send_all(PARTIAL, "space", send4, recv4)

    wait_all(SUM_YX, "yx", sumy_recv)
    sums = total(sumy_recv)
    sumb_send[...] = sums[0:16]
    send_all(SUM_BACK, "space", sumb_send, sumb_recv, each=False)
    out_bias[...] = jnp.sum(sums[16:24], axis=0, keepdims=True)

    wait_all(PARTIAL, "space", recv4)
    spectra = total(recv4).astype(bf16)
    u_rows = spectra[:, 0:C]
    d_wide = spectra[:, C:].astype(f32)
    row = lax.broadcasted_iota(jnp.int32, (16, C), 0)
    even = row % 2 == 0
    d_turned = jnp.where(even, pltpu.roll(d_wide, 15, 0), -pltpu.roll(d_wide, 1, 0))
    scale = jnp.where((row // 2 == 0) & (sp == 0), 1.0, 2.0).astype(f32) / (GRID * GRID)
    d_both = jnp.concatenate([d_wide, d_turned], axis=0).astype(bf16)
    back = jnp.zeros((16, C), f32)
    for k in range(N):
        product = dot_nt(d_both, weight[k])
        back = jnp.where(row // 2 == k, product[0:16, 0:C] + product[16:32, C:], back)
    send5[...] = (back * scale).astype(bf16)
    send_all(BACK, "space", send5, recv5, each=False)

    d_pair = jnp.concatenate([d_wide, d_turned], axis=1)
    row2 = lax.broadcasted_iota(jnp.int32, (16, 2 * C), 0)
    for k in range(N):
        chosen = jnp.where(row2 // 2 == k, d_pair, 0.0).astype(bf16)
        product = lax.dot_general(
            u_rows, chosen, (((0,), (0,)), ((), ())), preferred_element_type=f32
        )
        scale_k = (jnp.where(sp == 0, 1.0, 2.0) if k == 0 else 2.0) / (GRID * GRID)
        grads[k] = (product * scale_k).astype(bf16)
    store = []
    for part in range(2):
        copy = pltpu.make_async_copy(
            grads.at[:, :, pl.ds(part * C, C)], out_spec.at[0, :, part], out_sem.at[part]
        )
        copy.start()
        store.append(copy)

    wait_all(BACK, "space", recv5)
    send6[...] = dot(yt[1], recv5[...].reshape(2 * MODES, C)).astype(bf16).reshape(N, 16, C)
    send_all(BACK_YX, "yx", send6, recv6)
    wait_all(BACK_YX, "yx", recv6)
    send7[...] = dot(swap[...], recv6[...].reshape(2 * MODES, C)).astype(bf16).reshape(N, 16, C)
    send_all(BACK_Z, "z", send7, recv7)
    wait_all(BACK_Z, "z", recv7)

    send8[...] = dot(xtt[...], recv7[...].reshape(2 * MODES, C)).astype(bf16).reshape(N, MODES, C)
    send_all(ROWS, "space", send8, recv8)

    wait_all(SUM_BACK, "space", sumb_recv)
    out_local[...] = sumb_recv[...].reshape(C, C)

    wait_all(ROWS, "space", recv8)
    for t in range(N):
        rows_f[pl.ds(t, MODES, stride=N), :] = recv8[t].astype(f32) + local_part[t]
    out_grad[...] = rows_f[...].reshape(1, MODES, N, C).astype(bf16)

    for copy in store:
        copy.wait()
    for copy in started:
        copy.wait_send()


def on_device(field_in, pre_act, cotangent, spec_weight, local_weight):
    x_table, x_back, y_tables, swap = (jnp.asarray(t) for t in tables())
    wide = (N, 16, 2 * C)
    slim = (N, 16, C)
    anywhere = pl.BlockSpec(memory_space=pl.ANY)
    in_vmem = pl.BlockSpec(memory_space=pltpu.VMEM)
    grad_input, grad_spectral, grad_local, grad_bias = pl.pallas_call(
        kernel,
        out_shape=(
            jax.ShapeDtypeStruct((1, MODES, N, C), bf16),
            jax.ShapeDtypeStruct((1, N, 2, C, C), bf16),
            jax.ShapeDtypeStruct((C, C), f32),
            jax.ShapeDtypeStruct((1, C), f32),
        ),
        in_specs=[anywhere] * 9,
        out_specs=(in_vmem, anywhere, in_vmem, in_vmem),
        scratch_shapes=[
            pltpu.VMEM((MODES, N, C), bf16),
            pltpu.VMEM((MODES, N, C), bf16),
            pltpu.VMEM((MODES, N, C), bf16),
            pltpu.VMEM((N, 2 * C, C), bf16),
            pltpu.VMEM((C, C), bf16),
            pltpu.VMEM((2 * MODES, GRID), bf16),
            pltpu.VMEM((GRID, 2 * MODES), bf16),
            pltpu.VMEM((2, 2 * MODES, 2 * MODES), bf16),
            pltpu.VMEM((2 * MODES, 2 * MODES), bf16),
            pltpu.VMEM((GRID, C), f32),
            pltpu.VMEM((GRID, C), f32),
            pltpu.VMEM((N, MODES, 2 * C), bf16),
            pltpu.VMEM((N, MODES, 2 * C), bf16),
            pltpu.VMEM((N, MODES, C), f32),
            pltpu.VMEM(wide, bf16),
            pltpu.VMEM(wide, bf16),
            pltpu.VMEM(wide, bf16),
            pltpu.VMEM(wide, bf16),
            pltpu.VMEM(wide, f32),
            pltpu.VMEM(wide, f32),
            pltpu.VMEM((16, C), bf16),
            pltpu.VMEM(slim, bf16),
            pltpu.VMEM(slim, bf16),
            pltpu.VMEM(slim, bf16),
            pltpu.VMEM(slim, bf16),
            pltpu.VMEM(slim, bf16),
            pltpu.VMEM((N, MODES, C), bf16),
            pltpu.VMEM((N, MODES, C), bf16),
            pltpu.VMEM((N, 24, C), f32),
            pltpu.VMEM((N, 24, C), f32),
            pltpu.VMEM((24, C), f32),
            pltpu.VMEM((N, 24, C), f32),
            pltpu.VMEM((24, C), f32),
            pltpu.VMEM((N, 24, C), f32),
            pltpu.VMEM((16, C), f32),
            pltpu.VMEM((N, 16, C), f32),
            pltpu.VMEM((N, C, 2 * C), bf16),
            pltpu.SemaphoreType.DMA((9,)),
            pltpu.SemaphoreType.DMA((2,)),
            pltpu.SemaphoreType.DMA((12, N)),
            pltpu.SemaphoreType.DMA((12, N)),
        ],
        compiler_params=pltpu.CompilerParams(
            collective_id=0, has_side_effects=True, vmem_limit_bytes=32 * 1024 * 1024
        ),
        cost_estimate=pl.CostEstimate(
            flops=250_000_000, bytes_accessed=2_500_000, transcendentals=65536
        ),
    )(
        field_in, pre_act, cotangent, spec_weight.reshape(N, 2 * C, C), local_weight,
        x_table, x_back, y_tables, swap,
    )
    return grad_input, grad_spectral, grad_local, grad_bias.reshape(C)


def solution(mesh):
    placed = (
        P(None, "space", "dp", None),
        P(None, "space", "dp", None),
        P(None, "space", "dp", None),
        P("dp", "space", None, None, None),
        P(),
    )
    return jax.shard_map(
        on_device,
        mesh=mesh,
        in_specs=placed,
        out_specs=(P(None, "space", "dp", None), P("dp", "space", None, None, None), P(), P()),
        check_vma=False,
    )
```

```python
import math

import jax
import jax.numpy as jnp
import numpy as np
from jax import lax
from jax.experimental import pallas as pl
from jax.experimental.pallas import tpu as pltpu
from jax.sharding import PartitionSpec as P

root_two_pi = 0.7978845608028654
cubic_coef = 0.044715

N = 8
C = 128
GRID = 512
MODES = 64
COLS = 4
f32 = jnp.float32
bf16 = jnp.bfloat16

PARTIAL, BACK, SUM_SPACE, SUM_Z, SUM_YX, SUM_BACK = range(6)
FIELD, DELTA, ROWS, SPEC, GRAD = range(5)


def gelu_slope(values):
    tangent = jnp.tanh(root_two_pi * (values + cubic_coef * values * values * values))
    return 0.5 * (1.0 + tangent) + 0.5 * values * (1.0 - tangent * tangent) * root_two_pi * (
        1.0 + 3.0 * cubic_coef * values * values
    )


def trig(phases):
    angles = (phases % GRID).astype(np.float32) * np.float32(2.0 * math.pi / GRID)
    return np.cos(angles), np.sin(angles)


def tables():
    j = np.arange(MODES)
    frequency = np.where(j < MODES // 2, j, j - MODES)
    c, s = trig(frequency[:, None] * np.arange(GRID)[None, :])
    both = np.stack([c, s]).reshape(2, MODES, 4, 2 * MODES)
    x_table = both.transpose(2, 0, 1, 3).reshape(4, 2 * MODES, 2 * MODES)
    by_row = both.reshape(2, MODES, 4, 2, MODES).transpose(2, 3, 4, 1, 0)
    same = np.eye(COLS)
    x_back = np.einsum("hoxjp,tu->hotxjpu", by_row, same).reshape(4, GRID, GRID)
    y = np.arange(MODES)[None, :, None] * N + np.arange(2)[:, None, None] * COLS + np.arange(COLS)
    c, s = trig(np.arange(MODES)[None, :, None, None] * y[:, None])
    turn = np.stack([np.stack([c, -s], axis=-2), np.stack([-s, -c], axis=-2)], axis=2)
    y_table = np.einsum("okqdpt,fg->ofkqdgpt", turn, np.eye(2)).reshape(2, 4 * MODES, 2 * GRID)
    y_back = turn.transpose(0, 3, 4, 5, 1, 2).reshape(2, GRID, 2 * MODES)
    return [t.astype(bf16) for t in (x_table, y_table, y_back, x_back)]


def dot(a, b):
    return jnp.dot(a, b, preferred_element_type=f32)


def dot_nt(a, b):
    return lax.dot_general(a, b, (((1,), (1,)), ((), ())), preferred_element_type=f32)


def kernel(
    field_hbm, pre_hbm, cot_hbm, weight_hbm, lw_hbm, xt_hbm, yt_hbm, yb_hbm, xb_hbm,
    out_grad, out_spec, out_local, out_bias,
    field_v, pre_v, cot_v, weight, lw, xt, yt, yb, xb,
    rows_f, rows_d, local_part, swap_f, swap_d, held_f, held_d, stage,
    spec_send, spec_recv, part_send, part_recv, back_send, back_recv, grad_send, grad_recv,
    swap_rows, held_rows,
    sum_send, sum_recv, sumz_send, sumz_recv, sumy_send, sumy_recv, sumb_send, sumb_recv,
    grads, in_sem, out_sem, send_sem, recv_sem, wide_send, wide_recv,
):
    sp = lax.axis_index("space")
    dp = lax.axis_index("dp")
    yx = dp // N
    z = dp - yx * N
    row_chip = sp // 2
    core = sp - row_chip * 2
    twin = {"dp": dp, "space": row_chip * 2 + 1 - core}

    def peer(axis, o):
        if axis == "space":
            other = lax.rem(sp + o, N)
            return other, sp, {"dp": dp, "space": other}
        if axis == "z":
            other = lax.rem(z + o, N)
            return other, z, {"dp": yx * N + other, "space": sp}
        other = lax.rem(yx + o, N)
        return other, yx, {"dp": other * N + z, "space": sp}

    loads = []
    for i, (src, dst) in enumerate((
        (field_hbm.at[0], field_v), (pre_hbm.at[0], pre_v), (cot_hbm.at[0], cot_v),
        (xt_hbm.at[row_chip], xt), (lw_hbm, lw), (yt_hbm.at[core], yt),
        (weight_hbm, weight), (yb_hbm.at[core], yb), (xb_hbm.at[row_chip], xb),
    )):
        loads.append(pltpu.make_async_copy(src, dst, in_sem.at[i]))
        loads[-1].start()

    barrier = pltpu.get_barrier_semaphore()
    for o in range(1, N):
        pl.semaphore_signal(barrier, inc=1, device_id=peer("space", o)[2])

    def greet(o, carry):
        pl.semaphore_signal(
            barrier, inc=1, device_id={"dp": lax.rem(dp + o, MODES), "space": sp}
        )
        return carry

    lax.fori_loop(1, MODES, greet, 0)

    started = []

    def send_all(hop, axis, src, dst, each=True):
        for o in range(1, N):
            other, me, device = peer(axis, o)
            copy = pltpu.make_async_remote_copy(
                src_ref=src.at[other] if each else src,
                dst_ref=dst.at[me],
                send_sem=send_sem.at[hop, o],
                recv_sem=recv_sem.at[hop, me],
                device_id=device,
            )
            copy.start()
            started.append(copy)
        me = peer(axis, 0)[1]
        dst[me] = src[me] if each else src[...]

    def wait_all(hop, axis, dst):
        for o in range(1, N):
            other, me, device = peer(axis, o)
            pltpu.make_async_remote_copy(
                src_ref=dst.at[other],
                dst_ref=dst.at[other],
                send_sem=send_sem.at[hop, o],
                recv_sem=recv_sem.at[hop, other],
                device_id=device,
            ).wait_recv()

    def to_twin(hop, src, dst):
        copy = pltpu.make_async_remote_copy(
            src_ref=src, dst_ref=dst, send_sem=wide_send.at[hop], recv_sem=wide_recv.at[hop],
            device_id=twin,
        )
        copy.start()
        started.append(copy)
        return copy

    def to_all_dp(hop, src, dst):
        def step(o, carry):
            other = lax.rem(dp + o, MODES)
            pltpu.make_async_remote_copy(
                src_ref=src.at[other],
                dst_ref=dst.at[dp],
                send_sem=wide_send.at[hop],
                recv_sem=wide_recv.at[hop],
                device_id={"dp": other, "space": sp},
            ).start()
            return carry

        lax.fori_loop(1, MODES, step, 0)
        dst[dp] = src[dp]
        whole = pltpu.make_async_remote_copy(
            src_ref=src.at[pl.ds(0, MODES - 1)],
            dst_ref=dst.at[pl.ds(0, MODES - 1)],
            send_sem=wide_send.at[hop],
            recv_sem=wide_recv.at[hop],
            device_id={"dp": lax.rem(dp + 1, MODES), "space": sp},
        )
        started.append(whole)
        return whole

    def total(ref):
        acc = ref[0]
        for i in range(1, N):
            acc = acc + ref[i]
        return acc

    def split(rows, swap, held):
        for t in range(COLS):
            theirs = rows[pl.ds((1 - core) * COLS + t, MODES, stride=N), :]
            swap[:, t * C : (t + 1) * C] = theirs.astype(bf16)
        for t in range(COLS):
            mine = rows[pl.ds(core * COLS + t, MODES, stride=N), :]
            held[core, :, t * C : (t + 1) * C] = mine.astype(bf16)

    loads[0].wait()
    rows_f[...] = field_v[...].astype(f32).reshape(GRID, C)
    split(rows_f, swap_f, held_f)
    loads[1].wait()
    loads[2].wait()
    delta = (cot_v[...].astype(f32) * gelu_slope(pre_v[...].astype(f32))).astype(bf16)
    delta_wide = delta.astype(f32)
    rows_d[...] = delta_wide.reshape(GRID, C)
    split(rows_d, swap_d, held_d)
    pl.semaphore_wait(barrier, MODES - 1 + N - 1)
    field_copy = to_twin(FIELD, swap_f, held_f.at[core])
    delta_copy = to_twin(DELTA, swap_d, held_d.at[core])

    loads[3].wait()

    def transform(held, f):
        product = dot(xt[...], held[...].reshape(2 * MODES, COLS * C))
        for part in range(2):
            for t in range(COLS):
                stage[pl.ds(f * N + part * COLS + t, MODES, stride=2 * N), :] = product[
                    part * MODES : (part + 1) * MODES, t * C : (t + 1) * C
                ]

    field_copy.wait_recv()
    transform(held_f, 0)
    delta_copy.wait_recv()
    transform(held_d, 1)
    spec_send[...] = stage[...].astype(bf16).reshape(MODES, 2 * N, C)
    spec_copy = to_all_dp(SPEC, spec_send, spec_recv)

    field_rows = rows_f[...].astype(bf16)
    delta_rows = rows_d[...].astype(bf16)
    local = lax.dot_general(
        field_rows, delta_rows, (((0,), (0,)), ((), ())), preferred_element_type=f32
    )
    bias_part = jnp.sum(delta_wide, axis=0)
    for t in range(N):
        sum_send[t, 0:16, :] = local[16 * t : 16 * t + 16, :]
        sum_send[t, 16:24, :] = bias_part
    send_all(SUM_SPACE, "space", sum_send, sum_recv)
    for i in range(4, 9):
        loads[i].wait()
    local_part[...] = dot_nt(delta_rows, lw[...])

    spec_copy.wait_recv()
    product = dot(yt[...], spec_recv[...].reshape(2 * GRID, C))
    for f in range(2):
        part_send[:, f] = product[f * 2 * MODES : (f + 1) * 2 * MODES].reshape(N, 16, C)
    send_all(PARTIAL, "space", part_send, part_recv)

    wait_all(SUM_SPACE, "space", sum_recv)
    sumz_send[...] = total(sum_recv)
    send_all(SUM_Z, "z", sumz_send, sumz_recv, each=False)

    wait_all(PARTIAL, "space", part_recv)
    spectra = total(part_recv).astype(bf16)
    u_rows = spectra[0]
    d_wide = spectra[1].astype(f32)
    row = lax.broadcasted_iota(jnp.int32, (16, C), 0)
    even = row % 2 == 0
    d_turned = jnp.where(even, pltpu.roll(d_wide, 15, 0), -pltpu.roll(d_wide, 1, 0))
    scale = jnp.where((row // 2 == 0) & (sp == 0), 1.0, 2.0).astype(f32) / (GRID * GRID)
    d_both = jnp.concatenate([d_wide, d_turned], axis=0).astype(bf16)
    back = jnp.zeros((16, C), f32)
    for k in range(N):
        product = dot_nt(d_both, weight[k])
        back = jnp.where(row // 2 == k, product[0:16, 0:C] + product[16:32, C:], back)
    back_send[...] = (back * scale).astype(bf16)
    send_all(BACK, "space", back_send, back_recv, each=False)

    wait_all(SUM_Z, "z", sumz_recv)
    sumy_send[...] = total(sumz_recv)
    send_all(SUM_YX, "yx", sumy_send, sumy_recv, each=False)

    wait_all(BACK, "space", back_recv)
    grad_send[...] = dot(yb[...], back_recv[...].reshape(2 * MODES, C)).astype(bf16).reshape(MODES, N, C)
    grad_copy = to_all_dp(GRAD, grad_send, grad_recv)

    wait_all(SUM_YX, "yx", sumy_recv)
    sums = total(sumy_recv)
    sumb_send[...] = sums[0:16]
    send_all(SUM_BACK, "space", sumb_send, sumb_recv, each=False)
    out_bias[...] = jnp.sum(sums[16:24], axis=0, keepdims=True)

    d_pair = jnp.concatenate([d_wide, d_turned], axis=1)
    row2 = lax.broadcasted_iota(jnp.int32, (16, 2 * C), 0)
    for k in range(N):
        chosen = jnp.where(row2 // 2 == k, d_pair, 0.0).astype(bf16)
        product = lax.dot_general(
            u_rows, chosen, (((0,), (0,)), ((), ())), preferred_element_type=f32
        )
        scale_k = (jnp.where(sp == 0, 1.0, 2.0) if k == 0 else 2.0) / (GRID * GRID)
        for part in range(2):
            grads[k, part] = (product[:, part * C : (part + 1) * C] * scale_k).astype(bf16)
    store = pltpu.make_async_copy(grads, out_spec.at[0], out_sem.at[0])
    store.start()

    grad_copy.wait_recv()
    arrived = grad_recv[...].reshape(GRID, C)
    theirs = dot(xb[pl.ds((1 - core) * COLS * MODES, COLS * MODES), :], arrived)
    swap_rows[...] = theirs.astype(bf16).reshape(COLS, MODES, C)
    rows_copy = to_twin(ROWS, swap_rows, held_rows)
    mine = dot(xb[pl.ds(core * COLS * MODES, COLS * MODES), :], arrived)
    mine = mine.astype(bf16).astype(f32)
    for t in range(COLS):
        rows_f[pl.ds(core * COLS + t, MODES, stride=N), :] = mine[t * MODES : (t + 1) * MODES]

    wait_all(SUM_BACK, "space", sumb_recv)
    out_local[...] = sumb_recv[...].reshape(C, C)

    rows_copy.wait_recv()
    for t in range(COLS):
        rows_f[pl.ds((1 - core) * COLS + t, MODES, stride=N), :] = held_rows[t].astype(f32)
    out_grad[...] = (rows_f[...] + local_part[...]).reshape(1, MODES, N, C).astype(bf16)

    store.wait()
    for copy in started:
        copy.wait_send()


def finish(*refs):
    for i in range(4):
        refs[4 + i][...] = refs[i][...]


def on_device(field_in, pre_act, cotangent, spec_weight, local_weight):
    anywhere = pl.BlockSpec(memory_space=pl.ANY)
    in_vmem = pl.BlockSpec(memory_space=pltpu.VMEM)
    block = pltpu.VMEM((MODES, N, C), bf16)
    rows = pltpu.VMEM((GRID, C), f32)
    results = pl.pallas_call(
        kernel,
        out_shape=(
            jax.ShapeDtypeStruct((1, MODES, N, C), bf16),
            jax.ShapeDtypeStruct((1, N, 2, C, C), bf16),
            jax.ShapeDtypeStruct((C, C), f32),
            jax.ShapeDtypeStruct((1, C), f32),
        ),
        in_specs=[anywhere] * 9,
        out_specs=(in_vmem, anywhere, in_vmem, in_vmem),
        scratch_shapes=[
            block, block, block,
            pltpu.VMEM((N, 2 * C, C), bf16),
            pltpu.VMEM((C, C), bf16),
            pltpu.VMEM((2 * MODES, 2 * MODES), bf16),
            pltpu.VMEM((4 * MODES, 2 * GRID), bf16),
            pltpu.VMEM((GRID, 2 * MODES), bf16),
            pltpu.VMEM((GRID, GRID), bf16),
            rows, rows, rows,
            pltpu.VMEM((MODES, COLS * C), bf16),
            pltpu.VMEM((MODES, COLS * C), bf16),
            pltpu.VMEM((2, MODES, COLS * C), bf16),
            pltpu.VMEM((2, MODES, COLS * C), bf16),
            pltpu.VMEM((2 * GRID, C), f32),
            pltpu.VMEM((MODES, 2 * N, C), bf16),
            pltpu.VMEM((MODES, 2 * N, C), bf16),
            pltpu.VMEM((N, 2, 16, C), f32),
            pltpu.VMEM((N, 2, 16, C), f32),
            pltpu.VMEM((16, C), bf16),
            pltpu.VMEM((N, 16, C), bf16),
            block, block,
            pltpu.VMEM((COLS, MODES, C), bf16),
            pltpu.VMEM((COLS, MODES, C), bf16),
            pltpu.VMEM((N, 24, C), f32),
            pltpu.VMEM((N, 24, C), f32),
            pltpu.VMEM((24, C), f32),
            pltpu.VMEM((N, 24, C), f32),
            pltpu.VMEM((24, C), f32),
            pltpu.VMEM((N, 24, C), f32),
            pltpu.VMEM((16, C), f32),
            pltpu.VMEM((N, 16, C), f32),
            pltpu.VMEM((N, 2, C, C), bf16),
            pltpu.SemaphoreType.DMA((9,)),
            pltpu.SemaphoreType.DMA((1,)),
            pltpu.SemaphoreType.DMA((6, N)),
            pltpu.SemaphoreType.DMA((6, N)),
            pltpu.SemaphoreType.DMA((5,)),
            pltpu.SemaphoreType.DMA((5,)),
        ],
        compiler_params=pltpu.CompilerParams(
            collective_id=0, has_side_effects=True, vmem_limit_bytes=62 * 1024 * 1024
        ),
        cost_estimate=pl.CostEstimate(
            flops=250_000_000, bytes_accessed=2_500_000, transcendentals=65536
        ),
    )(
        field_in, pre_act, cotangent, spec_weight.reshape(N, 2 * C, C), local_weight,
        *(jnp.asarray(t) for t in tables()),
    )
    grad_input, grad_spectral, grad_local, grad_bias = pl.pallas_call(
        finish,
        out_shape=tuple(jax.ShapeDtypeStruct(r.shape, r.dtype) for r in results),
        in_specs=[in_vmem] * 4,
        out_specs=(in_vmem,) * 4,
        compiler_params=pltpu.CompilerParams(vmem_limit_bytes=62 * 1024 * 1024),
    )(*results)
    return grad_input, grad_spectral, grad_local, grad_bias.reshape(C)


def solution(mesh):
    placed = (
        P(None, "space", "dp", None),
        P(None, "space", "dp", None),
        P(None, "space", "dp", None),
        P("dp", "space", None, None, None),
        P(),
    )
    return jax.shard_map(
        on_device,
        mesh=mesh,
        in_specs=placed,
        out_specs=(P(None, "space", "dp", None), P("dp", "space", None, None, None), P(), P()),
        check_vma=False,
    )
```

```python
import math

import jax
import jax.numpy as jnp
import numpy as np
from jax import lax
from jax.experimental import pallas as pl
from jax.experimental.pallas import tpu as pltpu
from jax.sharding import PartitionSpec as P

root_two_pi = 0.7978845608028654
cubic_coef = 0.044715

N = 8
C = 128
GRID = 512
MODES = 64
COLS = 4
f32 = jnp.float32
bf16 = jnp.bfloat16

Z_ORDER = [4, 3, 5, 2, 6, 1, 7]
YX_ORDER = [(1, 2), (0, 2), (1, 1), (1, 3), (0, 1), (0, 3), (1, 0)]
SPACE_ORDER = [(2, 0), (2, 1), (1, 0), (3, 0), (1, 1), (3, 1), (0, 1)]
DP_ORDER = sorted(
    [(l, x, z) for l in range(2) for x in range(4) for z in range(8) if l or x or z],
    key=lambda o: -(o[0] + min(o[1], 4 - o[1]) + min(o[2], 8 - o[2])),
)
PARTIAL, BACK, SUM_SPACE, SUM_Z, SUM_YX, SUM_BACK = range(6)
FIELD, DELTA, ROWS, SPEC, GRAD = range(5)


def gelu_slope(values):
    tangent = jnp.tanh(root_two_pi * (values + cubic_coef * values * values * values))
    return 0.5 * (1.0 + tangent) + 0.5 * values * (1.0 - tangent * tangent) * root_two_pi * (
        1.0 + 3.0 * cubic_coef * values * values
    )


def trig(phases):
    angles = (phases % GRID).astype(np.float32) * np.float32(2.0 * math.pi / GRID)
    return np.cos(angles), np.sin(angles)


def tables():
    j = np.arange(MODES)
    frequency = np.where(j < MODES // 2, j, j - MODES)
    c, s = trig(frequency[:, None] * np.arange(GRID)[None, :])
    both = np.stack([c, s]).reshape(2, MODES, 4, 2 * MODES)
    x_table = both.transpose(2, 0, 1, 3).reshape(4, 2 * MODES, 2 * MODES)
    by_row = both.reshape(2, MODES, 4, 2, MODES).transpose(2, 3, 4, 1, 0)
    same = np.eye(COLS)
    x_back = np.einsum("hoxjp,tu->hotxjpu", by_row, same).reshape(4, GRID, GRID)
    y = np.arange(MODES)[None, :, None] * N + np.arange(2)[:, None, None] * COLS + np.arange(COLS)
    c, s = trig(np.arange(MODES)[None, :, None, None] * y[:, None])
    turn = np.stack([np.stack([c, -s], axis=-2), np.stack([-s, -c], axis=-2)], axis=2)
    y_table = np.einsum("okqdpt,fg->ofkqdgpt", turn, np.eye(2)).reshape(2, 4 * MODES, 2 * GRID)
    y_back = turn.transpose(0, 3, 4, 5, 1, 2).reshape(2, GRID, 2 * MODES)
    return [t.astype(bf16) for t in (x_table, y_table, y_back, x_back)]


def dot(a, b):
    return jnp.dot(a, b, preferred_element_type=f32)


def dot_nt(a, b):
    return lax.dot_general(a, b, (((1,), (1,)), ((), ())), preferred_element_type=f32)


def kernel(
    field_hbm, pre_hbm, cot_hbm, weight_hbm, lw_hbm, xt_hbm, yt_hbm, yb_hbm, xb_hbm,
    out_grad, out_spec, out_local, out_bias,
    field_v, pre_v, cot_v, weight, lw, xt, yt, yb, xb,
    rows_f, rows_d, local_part, swap_f, swap_d, held_f, held_d, stage,
    spec_send, spec_recv, part_send, part_recv, back_send, back_recv, grad_send, grad_recv,
    swap_rows, held_rows,
    sum_send, sum_recv, sumz_send, sumz_recv, sumy_send, sumy_recv, sumb_send, sumb_recv,
    in_sem, send_sem, recv_sem, wide_send, wide_recv, lines_in,
):
    sp = lax.axis_index("space")
    dp = lax.axis_index("dp")
    yx = dp // N
    z = dp - yx * N
    row_chip = sp // 2
    core = sp - row_chip * 2
    twin = {"dp": dp, "space": row_chip * 2 + 1 - core}

    def peer(axis, o):
        if axis == "space":
            chip, side = SPACE_ORDER[o - 1]
            other = lax.rem(row_chip + chip, 4) * 2 + lax.rem(core + side, 2)
            return other, sp, {"dp": dp, "space": other}
        if axis == "z":
            other = lax.rem(z + Z_ORDER[o - 1], N)
            return other, z, {"dp": yx * N + other, "space": sp}
        low, x = YX_ORDER[o - 1]
        other = lax.rem(yx // 4 + low, 2) * 4 + lax.rem(yx % 4 + x, 4)
        return other, yx, {"dp": other * N + z, "space": sp}

    def dp_peer(offset):
        low, x, deep = offset
        chips = lax.rem(yx // 4 + low, 2) * 4 + lax.rem(yx % 4 + x, 4)
        return chips * N + lax.rem(z + deep, N)

    loads = []
    for i, (src, dst) in enumerate((
        (field_hbm.at[0], field_v), (pre_hbm.at[0], pre_v), (cot_hbm.at[0], cot_v),
        (xt_hbm.at[row_chip], xt), (lw_hbm, lw), (yt_hbm.at[core], yt),
        (weight_hbm, weight), (yb_hbm.at[core], yb), (xb_hbm.at[row_chip], xb),
    )):
        loads.append(pltpu.make_async_copy(src, dst, in_sem.at[i]))
        loads[-1].start()

    barrier = pltpu.get_barrier_semaphore()
    for o in range(1, N):
        pl.semaphore_signal(barrier, inc=1, device_id=peer("space", o)[2])

    for o in range(1, N):
        for axis in ("z", "yx"):
            pl.semaphore_signal(barrier, inc=1, device_id=peer(axis, o)[2])

    started = []

    def send_all(hop, axis, src, dst, each=True):
        for o in range(1, N):
            other, me, device = peer(axis, o)
            copy = pltpu.make_async_remote_copy(
                src_ref=src.at[other] if each else src,
                dst_ref=dst.at[me],
                send_sem=send_sem.at[hop, o],
                recv_sem=recv_sem.at[hop, me],
                device_id=device,
            )
            copy.start()
            started.append(copy)
        me = {"space": sp, "z": z, "yx": yx}[axis]
        dst[me] = src[me] if each else src[...]

    def wait_all(hop, axis, dst):
        for o in range(1, N):
            other, me, device = peer(axis, o)
            pltpu.make_async_remote_copy(
                src_ref=dst.at[other],
                dst_ref=dst.at[other],
                send_sem=send_sem.at[hop, o],
                recv_sem=recv_sem.at[hop, other],
                device_id=device,
            ).wait_recv()

    def to_twin(hop, src, dst):
        copy = pltpu.make_async_remote_copy(
            src_ref=src, dst_ref=dst, send_sem=wide_send.at[hop], recv_sem=wide_recv.at[hop],
            device_id=twin,
        )
        copy.start()
        started.append(copy)
        return copy

    def to_all_dp(hop, src, dst):
        for offset in DP_ORDER:
            other = dp_peer(offset)
            pltpu.make_async_remote_copy(
                src_ref=src.at[other],
                dst_ref=dst.at[dp],
                send_sem=wide_send.at[hop],
                recv_sem=wide_recv.at[hop],
                device_id={"dp": other, "space": sp},
            ).start()
        dst[dp] = src[dp]
        whole = pltpu.make_async_remote_copy(
            src_ref=src.at[pl.ds(0, MODES - 1)],
            dst_ref=dst.at[pl.ds(0, MODES - 1)],
            send_sem=wide_send.at[hop],
            recv_sem=wide_recv.at[hop],
            device_id={"dp": lax.rem(dp + 1, MODES), "space": sp},
        )
        started.append(whole)
        return whole

    def total(ref):
        acc = ref[0]
        for i in range(1, N):
            acc = acc + ref[i]
        return acc

    def split(rows, swap, held):
        for t in range(COLS):
            theirs = rows[pl.ds((1 - core) * COLS + t, MODES, stride=N), :]
            swap[:, t * C : (t + 1) * C] = theirs.astype(bf16)
        for t in range(COLS):
            mine = rows[pl.ds(core * COLS + t, MODES, stride=N), :]
            held[core, :, t * C : (t + 1) * C] = mine.astype(bf16)

    loads[0].wait()
    rows_f[...] = field_v[...].astype(f32).reshape(GRID, C)
    split(rows_f, swap_f, held_f)
    loads[1].wait()
    loads[2].wait()
    delta = (cot_v[...].astype(f32) * gelu_slope(pre_v[...].astype(f32))).astype(bf16)
    delta_wide = delta.astype(f32)
    rows_d[...] = delta_wide.reshape(GRID, C)
    split(rows_d, swap_d, held_d)
    pl.semaphore_wait(barrier, 3 * (N - 1))
    for o in range(1, N):
        pl.semaphore_signal(lines_in, inc=1, device_id=peer("yx", o)[2])
    field_copy = to_twin(FIELD, swap_f, held_f.at[core])
    delta_copy = to_twin(DELTA, swap_d, held_d.at[core])

    loads[3].wait()

    def transform(held, f):
        product = dot(xt[...], held[...].reshape(2 * MODES, COLS * C))
        for part in range(2):
            for t in range(COLS):
                stage[pl.ds(f * N + part * COLS + t, MODES, stride=2 * N), :] = product[
                    part * MODES : (part + 1) * MODES, t * C : (t + 1) * C
                ]

    field_copy.wait_recv()
    transform(held_f, 0)
    delta_copy.wait_recv()
    transform(held_d, 1)
    spec_send[...] = stage[...].astype(bf16).reshape(MODES, 2 * N, C)
    pl.semaphore_wait(lines_in, N - 1)
    spec_copy = to_all_dp(SPEC, spec_send, spec_recv)

    field_rows = rows_f[...].astype(bf16)
    delta_rows = rows_d[...].astype(bf16)
    local = lax.dot_general(
        field_rows, delta_rows, (((0,), (0,)), ((), ())), preferred_element_type=f32
    )
    bias_part = jnp.sum(delta_wide, axis=0)
    for t in range(N):
        sum_send[t, 0:16, :] = local[16 * t : 16 * t + 16, :]
        sum_send[t, 16:24, :] = bias_part
    send_all(SUM_SPACE, "space", sum_send, sum_recv)
    for i in range(4, 9):
        loads[i].wait()
    local_part[...] = dot_nt(delta_rows, lw[...])

    spec_copy.wait_recv()
    product = dot(yt[...], spec_recv[...].reshape(2 * GRID, C))
    for f in range(2):
        part_send[:, f] = product[f * 2 * MODES : (f + 1) * 2 * MODES].reshape(N, 16, C)
    send_all(PARTIAL, "space", part_send, part_recv)

    wait_all(SUM_SPACE, "space", sum_recv)
    sumz_send[...] = total(sum_recv)
    send_all(SUM_Z, "z", sumz_send, sumz_recv, each=False)

    wait_all(PARTIAL, "space", part_recv)
    spectra = total(part_recv).astype(bf16)
    u_rows = spectra[0]
    d_wide = spectra[1].astype(f32)
    row = lax.broadcasted_iota(jnp.int32, (16, C), 0)
    even = row % 2 == 0
    d_turned = jnp.where(even, pltpu.roll(d_wide, 15, 0), -pltpu.roll(d_wide, 1, 0))
    scale = jnp.where((row // 2 == 0) & (sp == 0), 1.0, 2.0).astype(f32) / (GRID * GRID)
    d_both = jnp.concatenate([d_wide, d_turned], axis=0).astype(bf16)
    back = jnp.zeros((16, C), f32)
    for k in range(N):
        product = dot_nt(d_both, weight[k])
        back = jnp.where(row // 2 == k, product[0:16, 0:C] + product[16:32, C:], back)
    back_send[...] = (back * scale).astype(bf16)
    send_all(BACK, "space", back_send, back_recv, each=False)

    wait_all(SUM_Z, "z", sumz_recv)
    sumy_send[...] = total(sumz_recv)
    send_all(SUM_YX, "yx", sumy_send, sumy_recv, each=False)

    wait_all(BACK, "space", back_recv)
    grad_send[...] = dot(yb[...], back_recv[...].reshape(2 * MODES, C)).astype(bf16).reshape(MODES, N, C)
    grad_copy = to_all_dp(GRAD, grad_send, grad_recv)

    wait_all(SUM_YX, "yx", sumy_recv)
    sums = total(sumy_recv)
    sumb_send[...] = sums[0:16]
    send_all(SUM_BACK, "space", sumb_send, sumb_recv, each=False)
    out_bias[...] = jnp.sum(sums[16:24], axis=0, keepdims=True)

    d_pair = jnp.concatenate([d_wide, d_turned], axis=1)
    row2 = lax.broadcasted_iota(jnp.int32, (16, 2 * C), 0)
    for k in range(N):
        chosen = jnp.where(row2 // 2 == k, d_pair, 0.0).astype(bf16)
        product = lax.dot_general(
            u_rows, chosen, (((0,), (0,)), ((), ())), preferred_element_type=f32
        )
        scale_k = (jnp.where(sp == 0, 1.0, 2.0) if k == 0 else 2.0) / (GRID * GRID)
        for part in range(2):
            out_spec[0, k, part] = (product[:, part * C : (part + 1) * C] * scale_k).astype(bf16)


    grad_copy.wait_recv()
    arrived = grad_recv[...].reshape(GRID, C)
    theirs = dot(xb[pl.ds((1 - core) * COLS * MODES, COLS * MODES), :], arrived)
    swap_rows[...] = theirs.astype(bf16).reshape(COLS, MODES, C)
    rows_copy = to_twin(ROWS, swap_rows, held_rows)
    mine = dot(xb[pl.ds(core * COLS * MODES, COLS * MODES), :], arrived)
    mine = mine.astype(bf16).astype(f32)
    for t in range(COLS):
        rows_f[pl.ds(core * COLS + t, MODES, stride=N), :] = mine[t * MODES : (t + 1) * MODES]

    wait_all(SUM_BACK, "space", sumb_recv)
    out_local[...] = sumb_recv[...].reshape(C, C)

    rows_copy.wait_recv()
    for t in range(COLS):
        rows_f[pl.ds((1 - core) * COLS + t, MODES, stride=N), :] = held_rows[t].astype(f32)
    out_grad[...] = (rows_f[...] + local_part[...]).reshape(1, MODES, N, C).astype(bf16)

    for copy in started:
        copy.wait_send()


def hand_over(*refs):
    copies = [pltpu.make_async_copy(refs[i], refs[4 + i], refs[-1].at[i]) for i in range(4)]
    for copy in copies:
        copy.start()
    for copy in copies:
        copy.wait()


def on_device(field_in, pre_act, cotangent, spec_weight, local_weight):
    anywhere = pl.BlockSpec(memory_space=pl.ANY)
    in_vmem = pl.BlockSpec(memory_space=pltpu.VMEM)
    block = pltpu.VMEM((MODES, N, C), bf16)
    rows = pltpu.VMEM((GRID, C), f32)
    results = pl.pallas_call(
        kernel,
        out_shape=(
            pltpu.VMEM((1, MODES, N, C), bf16),
            pltpu.VMEM((1, N, 2, C, C), bf16),
            pltpu.VMEM((C, C), f32),
            pltpu.VMEM((1, C), f32),
        ),
        in_specs=[anywhere] * 9,
        out_specs=(in_vmem,) * 4,
        scratch_shapes=[
            block, block, block,
            pltpu.VMEM((N, 2 * C, C), bf16),
            pltpu.VMEM((C, C), bf16),
            pltpu.VMEM((2 * MODES, 2 * MODES), bf16),
            pltpu.VMEM((4 * MODES, 2 * GRID), bf16),
            pltpu.VMEM((GRID, 2 * MODES), bf16),
            pltpu.VMEM((GRID, GRID), bf16),
            rows, rows, rows,
            pltpu.VMEM((MODES, COLS * C), bf16),
            pltpu.VMEM((MODES, COLS * C), bf16),
            pltpu.VMEM((2, MODES, COLS * C), bf16),
            pltpu.VMEM((2, MODES, COLS * C), bf16),
            pltpu.VMEM((2 * GRID, C), f32),
            pltpu.VMEM((MODES, 2 * N, C), bf16),
            pltpu.VMEM((MODES, 2 * N, C), bf16),
            pltpu.VMEM((N, 2, 16, C), f32),
            pltpu.VMEM((N, 2, 16, C), f32),
            pltpu.VMEM((16, C), bf16),
            pltpu.VMEM((N, 16, C), bf16),
            block, block,
            pltpu.VMEM((COLS, MODES, C), bf16),
            pltpu.VMEM((COLS, MODES, C), bf16),
            pltpu.VMEM((N, 24, C), f32),
            pltpu.VMEM((N, 24, C), f32),
            pltpu.VMEM((24, C), f32),
            pltpu.VMEM((N, 24, C), f32),
            pltpu.VMEM((24, C), f32),
            pltpu.VMEM((N, 24, C), f32),
            pltpu.VMEM((16, C), f32),
            pltpu.VMEM((N, 16, C), f32),
            pltpu.SemaphoreType.DMA((9,)),
            pltpu.SemaphoreType.DMA((6, N)),
            pltpu.SemaphoreType.DMA((6, N)),
            pltpu.SemaphoreType.DMA((5,)),
            pltpu.SemaphoreType.DMA((5,)),
            pltpu.SemaphoreType.REGULAR,
        ],
        compiler_params=pltpu.CompilerParams(
            collective_id=0, has_side_effects=True, vmem_limit_bytes=int(62 * 1024 * 1024)
        ),
        cost_estimate=pl.CostEstimate(
            flops=250_000_000, bytes_accessed=2_500_000, transcendentals=65536
        ),
    )(
        field_in, pre_act, cotangent, spec_weight.reshape(N, 2 * C, C), local_weight,
        *(jnp.asarray(t) for t in tables()),
    )
    grad_input, grad_spectral, grad_local, grad_bias = pl.pallas_call(
        hand_over,
        out_shape=tuple(jax.ShapeDtypeStruct(r.shape, r.dtype) for r in results),
        in_specs=[in_vmem] * 4,
        out_specs=(anywhere,) * 4,
        scratch_shapes=[pltpu.SemaphoreType.DMA((4,))],
        compiler_params=pltpu.CompilerParams(vmem_limit_bytes=1024 * 1024),
    )(*results)
    return grad_input, grad_spectral, grad_local, grad_bias.reshape(C)


def solution(mesh):
    placed = (
        P(None, "space", "dp", None),
        P(None, "space", "dp", None),
        P(None, "space", "dp", None),
        P("dp", "space", None, None, None),
        P(),
    )
    return jax.shard_map(
        on_device,
        mesh=mesh,
        in_specs=placed,
        out_specs=(P(None, "space", "dp", None), P("dp", "space", None, None, None), P(), P()),
        check_vma=False,
    )
```

```python
import math

import jax
import jax.numpy as jnp
import numpy as np
from jax import lax
from jax.experimental import pallas as pl
from jax.experimental.pallas import tpu as pltpu
from jax.sharding import PartitionSpec as P

root_two_pi = 0.7978845608028654
cubic_coef = 0.044715

N = 8
C = 128
GRID = 512
MODES = 64
COLS = 4
f32 = jnp.float32
bf16 = jnp.bfloat16

Z_ORDER = [4, 3, 5, 2, 6, 1, 7]
YX_ORDER = [(1, 2), (0, 2), (1, 1), (1, 3), (0, 1), (0, 3), (1, 0)]
SPACE_ORDER = [(2, 0), (2, 1), (1, 0), (3, 0), (1, 1), (3, 1), (0, 1)]
DP_ORDER = sorted(
    [(l, x, z) for l in range(2) for x in range(4) for z in range(8) if l or x or z],
    key=lambda o: -(o[0] + min(o[1], 4 - o[1]) + min(o[2], 8 - o[2])),
)
PARTIAL, BACK, SUM_SPACE, SUM_Z, SUM_YX, SUM_BACK = range(6)
FIELD, DELTA, ROWS, SPEC, GRAD = range(5)


def gelu_slope(values):
    tangent = jnp.tanh(root_two_pi * (values + cubic_coef * values * values * values))
    return 0.5 * (1.0 + tangent) + 0.5 * values * (1.0 - tangent * tangent) * root_two_pi * (
        1.0 + 3.0 * cubic_coef * values * values
    )


def trig(phases):
    angles = (phases % GRID).astype(np.float32) * np.float32(2.0 * math.pi / GRID)
    return np.cos(angles), np.sin(angles)


def tables():
    j = np.arange(MODES)
    frequency = np.where(j < MODES // 2, j, j - MODES)
    c, s = trig(frequency[:, None] * np.arange(GRID)[None, :])
    both = np.stack([c, s]).reshape(2, MODES, 4, 2 * MODES)
    x_table = both.transpose(2, 0, 1, 3).reshape(4, 2 * MODES, 2 * MODES)
    by_row = both.reshape(2, MODES, 4, 2, MODES).transpose(2, 3, 4, 1, 0)
    same = np.eye(COLS)
    x_back = np.einsum("hoxjp,tu->hotxjpu", by_row, same).reshape(4, GRID, GRID)
    y = np.arange(MODES)[None, :, None] * N + np.arange(2)[:, None, None] * COLS + np.arange(COLS)
    c, s = trig(np.arange(MODES)[None, :, None, None] * y[:, None])
    turn = np.stack([np.stack([c, -s], axis=-2), np.stack([-s, -c], axis=-2)], axis=2)
    y_table = np.einsum("okqdpt,fg->ofkqdgpt", turn, np.eye(2)).reshape(2, 4 * MODES, 2 * GRID)
    y_back = turn.transpose(0, 3, 4, 5, 1, 2).reshape(2, GRID, 2 * MODES)
    return [t.astype(bf16) for t in (x_table, y_table, y_back, x_back)]


def dot(a, b):
    return jnp.dot(a, b, preferred_element_type=f32)


def dot_nt(a, b):
    return lax.dot_general(a, b, (((1,), (1,)), ((), ())), preferred_element_type=f32)


def kernel(
    field_hbm, pre_hbm, cot_hbm, weight_hbm, lw_hbm, xt_hbm, yt_hbm, yb_hbm, xb_hbm,
    out_grad, out_spec, out_local, out_bias,
    field_v, pre_v, cot_v, weight, turned, lw, xt, yt, yb, xb,
    rows_f, rows_d, local_part, swap_f, swap_d, held_f, held_d, stage,
    spec_send, spec_recv, part_send, part_recv, back_send, back_recv, grad_send, grad_recv,
    swap_rows, held_rows,
    sum_send, sum_recv, sumz_send, sumz_recv, sumy_send, sumy_recv, sumb_send, sumb_recv,
    in_sem, send_sem, recv_sem, wide_send, wide_recv, lines_in,
):
    sp = lax.axis_index("space")
    dp = lax.axis_index("dp")
    yx = dp // N
    z = dp - yx * N
    row_chip = sp // 2
    core = sp - row_chip * 2
    twin = {"dp": dp, "space": row_chip * 2 + 1 - core}

    def peer(axis, o):
        if axis == "space":
            chip, side = SPACE_ORDER[o - 1]
            other = lax.rem(row_chip + chip, 4) * 2 + lax.rem(core + side, 2)
            return other, sp, {"dp": dp, "space": other}
        if axis == "z":
            other = lax.rem(z + Z_ORDER[o - 1], N)
            return other, z, {"dp": yx * N + other, "space": sp}
        low, x = YX_ORDER[o - 1]
        other = lax.rem(yx // 4 + low, 2) * 4 + lax.rem(yx % 4 + x, 4)
        return other, yx, {"dp": other * N + z, "space": sp}

    def dp_peer(offset):
        low, x, deep = offset
        chips = lax.rem(yx // 4 + low, 2) * 4 + lax.rem(yx % 4 + x, 4)
        return chips * N + lax.rem(z + deep, N)

    loads = []
    for i, (src, dst) in enumerate((
        (field_hbm.at[0], field_v), (pre_hbm.at[0], pre_v), (cot_hbm.at[0], cot_v),
        (xt_hbm.at[row_chip], xt), (lw_hbm, lw), (yt_hbm.at[core], yt),
        (weight_hbm, weight), (yb_hbm.at[core], yb), (xb_hbm.at[row_chip], xb),
    )):
        loads.append(pltpu.make_async_copy(src, dst, in_sem.at[i]))
    for load in loads[:3]:
        load.start()

    barrier = pltpu.get_barrier_semaphore()
    for axis in ("z", "yx", "space"):
        for o in range(1, N):
            pl.semaphore_signal(barrier, inc=1, device_id=peer(axis, o)[2])
    for load in loads[3:]:
        load.start()

    started = []

    def send_all(hop, axis, src, dst, each=True):
        for o in range(1, N):
            other, me, device = peer(axis, o)
            copy = pltpu.make_async_remote_copy(
                src_ref=src.at[other] if each else src,
                dst_ref=dst.at[me],
                send_sem=send_sem.at[hop, o],
                recv_sem=recv_sem.at[hop],
                device_id=device,
            )
            copy.start()
            started.append(copy)
        me = {"space": sp, "z": z, "yx": yx}[axis]
        dst[me] = src[me] if each else src[...]

    def wait_all(hop, axis, dst):
        seven = dst.at[pl.ds(0, N - 1)]
        pltpu.make_async_remote_copy(
            src_ref=seven,
            dst_ref=seven,
            send_sem=send_sem.at[hop, 0],
            recv_sem=recv_sem.at[hop],
            device_id=twin,
        ).wait_recv()

    def to_twin(hop, src, dst):
        copy = pltpu.make_async_remote_copy(
            src_ref=src, dst_ref=dst, send_sem=wide_send.at[hop], recv_sem=wide_recv.at[hop],
            device_id=twin,
        )
        copy.start()
        started.append(copy)
        return copy

    def to_all_dp(hop, src, dst, before_others=None):
        on_lines = lambda o: o[2] == 0 or o[:2] == (0, 0)
        order = DP_ORDER if before_others is None else sorted(DP_ORDER, key=lambda o: not on_lines(o))
        for place, offset in enumerate(order):
            if before_others is not None and place == 2 * (N - 1):
                before_others()
            other = dp_peer(offset)
            pltpu.make_async_remote_copy(
                src_ref=src.at[other],
                dst_ref=dst.at[dp],
                send_sem=wide_send.at[hop],
                recv_sem=wide_recv.at[hop],
                device_id={"dp": other, "space": sp},
            ).start()
        dst[dp] = src[dp]
        whole = pltpu.make_async_remote_copy(
            src_ref=src.at[pl.ds(0, MODES - 1)],
            dst_ref=dst.at[pl.ds(0, MODES - 1)],
            send_sem=wide_send.at[hop],
            recv_sem=wide_recv.at[hop],
            device_id={"dp": lax.rem(dp + 1, MODES), "space": sp},
        )
        started.append(whole)
        return whole

    def total(ref):
        acc = ref[0]
        for i in range(1, N):
            acc = acc + ref[i]
        return acc

    def split(rows, swap, held):
        for t in range(COLS):
            theirs = rows[pl.ds((1 - core) * COLS + t, MODES, stride=N), :]
            swap[:, t * C : (t + 1) * C] = theirs.astype(bf16)
        for t in range(COLS):
            mine = rows[pl.ds(core * COLS + t, MODES, stride=N), :]
            held[core, :, t * C : (t + 1) * C] = mine.astype(bf16)

    loads[0].wait()
    rows_f[...] = field_v[...].astype(f32).reshape(GRID, C)
    split(rows_f, swap_f, held_f)
    loads[1].wait()
    loads[2].wait()
    delta = (cot_v[...].astype(f32) * gelu_slope(pre_v[...].astype(f32))).astype(bf16)
    delta_wide = delta.astype(f32)
    rows_d[...] = delta_wide.reshape(GRID, C)
    split(rows_d, swap_d, held_d)
    pl.semaphore_wait(barrier, 3 * (N - 1))
    field_copy = to_twin(FIELD, swap_f, held_f.at[core])
    delta_copy = to_twin(DELTA, swap_d, held_d.at[core])
    for o in range(1, N):
        pl.semaphore_signal(lines_in, inc=1, device_id=peer("yx", o)[2])

    loads[3].wait()

    def transform(held, f):
        product = dot(xt[...], held[...].reshape(2 * MODES, COLS * C))
        for part in range(2):
            for t in range(COLS):
                stage[pl.ds(f * N + part * COLS + t, MODES, stride=2 * N), :] = product[
                    part * MODES : (part + 1) * MODES, t * C : (t + 1) * C
                ]

    field_copy.wait_recv()
    transform(held_f, 0)
    delta_copy.wait_recv()
    transform(held_d, 1)
    spec_send[...] = stage[...].astype(bf16).reshape(MODES, 2 * N, C)
    spec_copy = to_all_dp(
        SPEC, spec_send, spec_recv, lambda: pl.semaphore_wait(lines_in, N - 1)
    )

    field_rows = rows_f[...].astype(bf16)
    delta_rows = rows_d[...].astype(bf16)
    local = lax.dot_general(
        field_rows, delta_rows, (((0,), (0,)), ((), ())), preferred_element_type=f32
    )
    bias_part = jnp.sum(delta_wide, axis=0)
    for t in range(N):
        sum_send[t, 0:16, :] = local[16 * t : 16 * t + 16, :]
        sum_send[t, 16:24, :] = bias_part
    send_all(SUM_SPACE, "space", sum_send, sum_recv)
    for i in range(4, 9):
        loads[i].wait()
    local_part[...] = dot_nt(delta_rows, lw[...])
    for k in range(N):
        turned[k] = weight[k].T

    spec_copy.wait_recv()
    product = dot(yt[...], spec_recv[...].reshape(2 * GRID, C))
    for f in range(2):
        part_send[:, f] = product[f * 2 * MODES : (f + 1) * 2 * MODES].reshape(N, 16, C)
    send_all(PARTIAL, "space", part_send, part_recv)

    wait_all(SUM_SPACE, "space", sum_recv)
    sumz_send[...] = total(sum_recv)
    send_all(SUM_Z, "z", sumz_send, sumz_recv, each=False)

    wait_all(PARTIAL, "space", part_recv)
    spectra = total(part_recv).astype(bf16)
    u_rows = spectra[0]
    d_wide = spectra[1].astype(f32)
    row = lax.broadcasted_iota(jnp.int32, (16, C), 0)
    even = row % 2 == 0
    d_turned = jnp.where(even, pltpu.roll(d_wide, 15, 0), -pltpu.roll(d_wide, 1, 0))
    scale = jnp.where((row // 2 == 0) & (sp == 0), 1.0, 2.0).astype(f32) / (GRID * GRID)
    d_both = jnp.concatenate([d_wide, d_turned], axis=0).astype(bf16)
    back = jnp.zeros((16, C), f32)
    for k in range(N):
        product = dot(d_both, turned[k])
        back = jnp.where(row // 2 == k, product[0:16, 0:C] + product[16:32, C:], back)
    back_send[...] = (back * scale).astype(bf16)
    send_all(BACK, "space", back_send, back_recv, each=False)

    wait_all(SUM_Z, "z", sumz_recv)
    sumy_send[...] = total(sumz_recv)
    send_all(SUM_YX, "yx", sumy_send, sumy_recv, each=False)

    wait_all(BACK, "space", back_recv)
    grad_send[...] = dot(yb[...], back_recv[...].reshape(2 * MODES, C)).astype(bf16).reshape(MODES, N, C)
    grad_copy = to_all_dp(GRAD, grad_send, grad_recv)

    wait_all(SUM_YX, "yx", sumy_recv)
    sums = total(sumy_recv)
    sumb_send[...] = sums[0:16]
    send_all(SUM_BACK, "space", sumb_send, sumb_recv, each=False)
    out_bias[...] = jnp.sum(sums[16:24], axis=0, keepdims=True)

    d_pair = jnp.concatenate([d_wide, d_turned], axis=1)
    row2 = lax.broadcasted_iota(jnp.int32, (16, 2 * C), 0)
    for k in range(N):
        chosen = jnp.where(row2 // 2 == k, d_pair, 0.0).astype(bf16)
        product = lax.dot_general(
            u_rows, chosen, (((0,), (0,)), ((), ())), preferred_element_type=f32
        )
        scale_k = (jnp.where(sp == 0, 1.0, 2.0) if k == 0 else 2.0) / (GRID * GRID)
        for part in range(2):
            out_spec[0, k, part] = (product[:, part * C : (part + 1) * C] * scale_k).astype(bf16)


    grad_copy.wait_recv()
    arrived = grad_recv[...].reshape(GRID, C)
    theirs = dot(xb[pl.ds((1 - core) * COLS * MODES, COLS * MODES), :], arrived)
    swap_rows[...] = theirs.astype(bf16).reshape(COLS, MODES, C)
    rows_copy = to_twin(ROWS, swap_rows, held_rows)
    mine = dot(xb[pl.ds(core * COLS * MODES, COLS * MODES), :], arrived)
    mine = mine.astype(bf16).astype(f32)
    for t in range(COLS):
        rows_f[pl.ds(core * COLS + t, MODES, stride=N), :] = mine[t * MODES : (t + 1) * MODES]

    wait_all(SUM_BACK, "space", sumb_recv)
    out_local[...] = sumb_recv[...].reshape(C, C)

    rows_copy.wait_recv()
    for t in range(COLS):
        rows_f[pl.ds((1 - core) * COLS + t, MODES, stride=N), :] = held_rows[t].astype(f32)
    out_grad[...] = (rows_f[...] + local_part[...]).reshape(1, MODES, N, C).astype(bf16)

    for copy in started:
        copy.wait_send()


def hand_over(*refs):
    copies = [pltpu.make_async_copy(refs[i], refs[4 + i], refs[-1].at[i]) for i in range(4)]
    for copy in copies:
        copy.start()
    for copy in copies:
        copy.wait()


def on_device(field_in, pre_act, cotangent, spec_weight, local_weight):
    anywhere = pl.BlockSpec(memory_space=pl.ANY)
    in_vmem = pl.BlockSpec(memory_space=pltpu.VMEM)
    block = pltpu.VMEM((MODES, N, C), bf16)
    rows = pltpu.VMEM((GRID, C), f32)
    results = pl.pallas_call(
        kernel,
        out_shape=(
            pltpu.VMEM((1, MODES, N, C), bf16),
            pltpu.VMEM((1, N, 2, C, C), bf16),
            pltpu.VMEM((C, C), f32),
            pltpu.VMEM((1, C), f32),
        ),
        in_specs=[anywhere] * 9,
        out_specs=(in_vmem,) * 4,
        scratch_shapes=[
            block, block, block,
            pltpu.VMEM((N, 2 * C, C), bf16),
            pltpu.VMEM((N, C, 2 * C), bf16),
            pltpu.VMEM((C, C), bf16),
            pltpu.VMEM((2 * MODES, 2 * MODES), bf16),
            pltpu.VMEM((4 * MODES, 2 * GRID), bf16),
            pltpu.VMEM((GRID, 2 * MODES), bf16),
            pltpu.VMEM((GRID, GRID), bf16),
            rows, rows, rows,
            pltpu.VMEM((MODES, COLS * C), bf16),
            pltpu.VMEM((MODES, COLS * C), bf16),
            pltpu.VMEM((2, MODES, COLS * C), bf16),
            pltpu.VMEM((2, MODES, COLS * C), bf16),
            pltpu.VMEM((2 * GRID, C), f32),
            pltpu.VMEM((MODES, 2 * N, C), bf16),
            pltpu.VMEM((MODES, 2 * N, C), bf16),
            pltpu.VMEM((N, 2, 16, C), f32),
            pltpu.VMEM((N, 2, 16, C), f32),
            pltpu.VMEM((16, C), bf16),
            pltpu.VMEM((N, 16, C), bf16),
            block, block,
            pltpu.VMEM((COLS, MODES, C), bf16),
            pltpu.VMEM((COLS, MODES, C), bf16),
            pltpu.VMEM((N, 24, C), f32),
            pltpu.VMEM((N, 24, C), f32),
            pltpu.VMEM((24, C), f32),
            pltpu.VMEM((N, 24, C), f32),
            pltpu.VMEM((24, C), f32),
            pltpu.VMEM((N, 24, C), f32),
            pltpu.VMEM((16, C), f32),
            pltpu.VMEM((N, 16, C), f32),
            pltpu.SemaphoreType.DMA((9,)),
            pltpu.SemaphoreType.DMA((6, N)),
            pltpu.SemaphoreType.DMA((6,)),
            pltpu.SemaphoreType.DMA((5,)),
            pltpu.SemaphoreType.DMA((5,)),
            pltpu.SemaphoreType.REGULAR,
        ],
        compiler_params=pltpu.CompilerParams(
            collective_id=0, has_side_effects=True, vmem_limit_bytes=int(62 * 1024 * 1024)
        ),
        cost_estimate=pl.CostEstimate(
            flops=250_000_000, bytes_accessed=2_500_000, transcendentals=65536
        ),
    )(
        field_in, pre_act, cotangent, spec_weight.reshape(N, 2 * C, C), local_weight,
        *(jnp.asarray(t) for t in tables()),
    )
    grad_input, grad_spectral, grad_local, grad_bias = pl.pallas_call(
        hand_over,
        out_shape=tuple(jax.ShapeDtypeStruct(r.shape, r.dtype) for r in results),
        in_specs=[in_vmem] * 4,
        out_specs=(anywhere,) * 4,
        scratch_shapes=[pltpu.SemaphoreType.DMA((4,))],
        compiler_params=pltpu.CompilerParams(vmem_limit_bytes=1024 * 1024),
    )(*results)
    return grad_input, grad_spectral, grad_local, grad_bias.reshape(C)


def solution(mesh):
    placed = (
        P(None, "space", "dp", None),
        P(None, "space", "dp", None),
        P(None, "space", "dp", None),
        P("dp", "space", None, None, None),
        P(),
    )
    return jax.shard_map(
        on_device,
        mesh=mesh,
        in_specs=placed,
        out_specs=(P(None, "space", "dp", None), P("dp", "space", None, None, None), P(), P()),
        check_vma=False,
    )
```

```python
import math

import jax
import jax.numpy as jnp
import numpy as np
from jax import lax
from jax.experimental import pallas as pl
from jax.experimental.pallas import tpu as pltpu
from jax.sharding import PartitionSpec as P

root_two_pi = 0.7978845608028654
cubic_coef = 0.044715

N = 8
C = 128
GRID = 512
MODES = 64
COLS = 4
f32 = jnp.float32
bf16 = jnp.bfloat16

Z_ORDER = [4, 3, 5, 2, 6, 1, 7]
YX_ORDER = [(1, 2), (0, 2), (1, 1), (1, 3), (0, 1), (0, 3), (1, 0)]
SPACE_ORDER = [(2, 0), (2, 1), (1, 0), (3, 0), (1, 1), (3, 1), (0, 1)]
DP_ORDER = sorted(
    [(l, x, z) for l in range(2) for x in range(4) for z in range(8) if l or x or z],
    key=lambda o: -(o[0] + min(o[1], 4 - o[1]) + min(o[2], 8 - o[2])),
)
PARTIAL, BACK, SUM_SPACE, SUM_Z, SUM_YX, SUM_BACK = range(6)
FIELD, DELTA, ROWS, SPEC, GRAD = range(5)


def gelu_slope(values):
    tangent = jnp.tanh(root_two_pi * (values + cubic_coef * values * values * values))
    return 0.5 * (1.0 + tangent) + 0.5 * values * (1.0 - tangent * tangent) * root_two_pi * (
        1.0 + 3.0 * cubic_coef * values * values
    )


def trig(phases):
    angles = (phases % GRID).astype(np.float32) * np.float32(2.0 * math.pi / GRID)
    return np.cos(angles), np.sin(angles)


def tables():
    j = np.arange(MODES)
    frequency = np.where(j < MODES // 2, j, j - MODES)
    c, s = trig(frequency[:, None] * np.arange(GRID)[None, :])
    both = np.stack([c, s]).reshape(2, MODES, 4, 2 * MODES)
    x_table = both.transpose(2, 0, 1, 3).reshape(4, 2 * MODES, 2 * MODES)
    by_row = both.reshape(2, MODES, 4, 2, MODES).transpose(2, 3, 4, 1, 0)
    same = np.eye(COLS)
    x_back = np.einsum("hoxjp,tu->hotxjpu", by_row, same).reshape(4, GRID, GRID)
    y = np.arange(MODES)[None, :, None] * N + np.arange(2)[:, None, None] * COLS + np.arange(COLS)
    c, s = trig(np.arange(MODES)[None, :, None, None] * y[:, None])
    turn = np.stack([np.stack([c, -s], axis=-2), np.stack([-s, -c], axis=-2)], axis=2)
    y_table = np.einsum("okqdpt,fg->ofkqdgpt", turn, np.eye(2)).reshape(2, 4 * MODES, 2 * GRID)
    y_back = turn.transpose(0, 3, 4, 5, 1, 2).reshape(2, GRID, 2 * MODES)
    return [t.astype(bf16) for t in (x_table, y_table, y_back, x_back)]


def dot(a, b):
    return jnp.dot(a, b, preferred_element_type=f32)


def dot_nt(a, b):
    return lax.dot_general(a, b, (((1,), (1,)), ((), ())), preferred_element_type=f32)


def kernel(
    field_hbm, pre_hbm, cot_hbm, weight_hbm, lw_hbm, xt_hbm, yt_hbm, yb_hbm, xb_hbm,
    out_grad, out_spec, out_local, out_bias,
    field_v, pre_v, cot_v, weight, turned, lw, xt, yt, yb, xb,
    rows_f, rows_d, local_part, swap_f, swap_d, held_f, held_d, stage,
    spec_send, spec_recv, part_send, part_recv, back_send, back_recv, grad_send, grad_recv,
    swap_rows, held_rows,
    sum_send, sum_recv, sumz_send, sumz_recv, sumy_send, sumy_recv, sumb_send, sumb_recv,
    in_sem, send_sem, recv_sem, wide_send, wide_recv, lines_in,
):
    sp = lax.axis_index("space")
    dp = lax.axis_index("dp")
    yx = dp // N
    z = dp - yx * N
    row_chip = sp // 2
    core = sp - row_chip * 2
    twin = {"dp": dp, "space": row_chip * 2 + 1 - core}

    def peer(axis, o):
        if axis == "space":
            chip, side = SPACE_ORDER[o - 1]
            other = lax.rem(row_chip + chip, 4) * 2 + lax.rem(core + side, 2)
            return other, sp, {"dp": dp, "space": other}
        if axis == "z":
            other = lax.rem(z + Z_ORDER[o - 1], N)
            return other, z, {"dp": yx * N + other, "space": sp}
        low, x = YX_ORDER[o - 1]
        other = lax.rem(yx // 4 + low, 2) * 4 + lax.rem(yx % 4 + x, 4)
        return other, yx, {"dp": other * N + z, "space": sp}

    def dp_peer(offset):
        low, x, deep = offset
        chips = lax.rem(yx // 4 + low, 2) * 4 + lax.rem(yx % 4 + x, 4)
        return chips * N + lax.rem(z + deep, N)

    loads = []
    for i, (src, dst) in enumerate((
        (field_hbm.at[0], field_v), (pre_hbm.at[0], pre_v), (cot_hbm.at[0], cot_v),
        (xt_hbm.at[row_chip], xt), (lw_hbm, lw), (yt_hbm.at[core], yt),
        (weight_hbm, weight), (yb_hbm.at[core], yb), (xb_hbm.at[row_chip], xb),
    )):
        loads.append(pltpu.make_async_copy(src, dst, in_sem.at[i]))
    for load in loads[:3]:
        load.start()

    barrier = pltpu.get_barrier_semaphore()
    for axis in ("z", "yx", "space"):
        for o in range(1, N):
            pl.semaphore_signal(barrier, inc=1, device_id=peer(axis, o)[2])
    for load in loads[3:]:
        load.start()

    started = []

    def drain():
        while started:
            started.pop(0).wait_send()


    def send_all(hop, axis, src, dst, each=True):
        for o in range(1, N):
            other, me, device = peer(axis, o)
            copy = pltpu.make_async_remote_copy(
                src_ref=src.at[other] if each else src,
                dst_ref=dst.at[me],
                send_sem=send_sem.at[hop],
                recv_sem=recv_sem.at[hop],
                device_id=device,
            )
            copy.start()
        seven = dst.at[pl.ds(0, N - 1)]
        started.append(pltpu.make_async_remote_copy(
            src_ref=seven,
            dst_ref=seven,
            send_sem=send_sem.at[hop],
            recv_sem=recv_sem.at[hop],
            device_id=twin,
        ))
        me = {"space": sp, "z": z, "yx": yx}[axis]
        dst[me] = src[me] if each else src[...]

    def wait_all(hop, axis, dst):
        seven = dst.at[pl.ds(0, N - 1)]
        pltpu.make_async_remote_copy(
            src_ref=seven,
            dst_ref=seven,
            send_sem=send_sem.at[hop],
            recv_sem=recv_sem.at[hop],
            device_id=twin,
        ).wait_recv()

    def to_twin(hop, src, dst):
        copy = pltpu.make_async_remote_copy(
            src_ref=src, dst_ref=dst, send_sem=wide_send.at[hop], recv_sem=wide_recv.at[hop],
            device_id=twin,
        )
        copy.start()
        started.append(copy)
        return copy

    def to_all_dp(hop, src, dst, before_others=None):
        on_lines = lambda o: o[2] == 0 or o[:2] == (0, 0)
        order = DP_ORDER if before_others is None else sorted(DP_ORDER, key=lambda o: not on_lines(o))
        for place, offset in enumerate(order):
            if before_others is not None and place == 2 * (N - 1):
                before_others()
            other = dp_peer(offset)
            pltpu.make_async_remote_copy(
                src_ref=src.at[other],
                dst_ref=dst.at[dp],
                send_sem=wide_send.at[hop],
                recv_sem=wide_recv.at[hop],
                device_id={"dp": other, "space": sp},
            ).start()
        dst[dp] = src[dp]
        whole = pltpu.make_async_remote_copy(
            src_ref=src.at[pl.ds(0, MODES - 1)],
            dst_ref=dst.at[pl.ds(0, MODES - 1)],
            send_sem=wide_send.at[hop],
            recv_sem=wide_recv.at[hop],
            device_id={"dp": lax.rem(dp + 1, MODES), "space": sp},
        )
        started.append(whole)
        return whole

    def total(ref):
        acc = ref[0]
        for i in range(1, N):
            acc = acc + ref[i]
        return acc

    def split(rows, swap, held):
        for t in range(COLS):
            theirs = rows[pl.ds((1 - core) * COLS + t, MODES, stride=N), :]
            swap[:, t * C : (t + 1) * C] = theirs.astype(bf16)
        for t in range(COLS):
            mine = rows[pl.ds(core * COLS + t, MODES, stride=N), :]
            held[core, :, t * C : (t + 1) * C] = mine.astype(bf16)

    loads[0].wait()
    rows_f[...] = field_v[...].astype(f32).reshape(GRID, C)
    split(rows_f, swap_f, held_f)
    loads[1].wait()
    loads[2].wait()
    delta = (cot_v[...].astype(f32) * gelu_slope(pre_v[...].astype(f32))).astype(bf16)
    delta_wide = delta.astype(f32)
    rows_d[...] = delta_wide.reshape(GRID, C)
    split(rows_d, swap_d, held_d)
    pl.semaphore_wait(barrier, 3 * (N - 1))
    field_copy = to_twin(FIELD, swap_f, held_f.at[core])
    delta_copy = to_twin(DELTA, swap_d, held_d.at[core])
    for o in range(1, N):
        pl.semaphore_signal(lines_in, inc=1, device_id=peer("yx", o)[2])

    loads[3].wait()

    def transform(held, f):
        product = dot(xt[...], held[...].reshape(2 * MODES, COLS * C))
        for part in range(2):
            for t in range(COLS):
                stage[pl.ds(f * N + part * COLS + t, MODES, stride=2 * N), :] = product[
                    part * MODES : (part + 1) * MODES, t * C : (t + 1) * C
                ]

    field_copy.wait_recv()
    transform(held_f, 0)
    delta_copy.wait_recv()
    transform(held_d, 1)
    spec_send[...] = stage[...].astype(bf16).reshape(MODES, 2 * N, C)
    spec_copy = to_all_dp(
        SPEC, spec_send, spec_recv, lambda: pl.semaphore_wait(lines_in, N - 1)
    )

    field_rows = rows_f[...].astype(bf16)
    delta_rows = rows_d[...].astype(bf16)
    local = lax.dot_general(
        field_rows, delta_rows, (((0,), (0,)), ((), ())), preferred_element_type=f32
    )
    bias_part = jnp.sum(delta_wide, axis=0)
    for t in range(N):
        sum_send[t, 0:16, :] = local[16 * t : 16 * t + 16, :]
        sum_send[t, 16:24, :] = bias_part
    send_all(SUM_SPACE, "space", sum_send, sum_recv)
    for i in range(4, 9):
        loads[i].wait()
    local_part[...] = dot_nt(delta_rows, lw[...])
    for k in range(N):
        turned[k] = weight[k].T

    spec_copy.wait_recv()
    product = dot(yt[...], spec_recv[...].reshape(2 * GRID, C))
    for f in range(2):
        part_send[:, f] = product[f * 2 * MODES : (f + 1) * 2 * MODES].reshape(N, 16, C)
    send_all(PARTIAL, "space", part_send, part_recv)

    wait_all(SUM_SPACE, "space", sum_recv)
    sumz_send[...] = total(sum_recv)
    send_all(SUM_Z, "z", sumz_send, sumz_recv, each=False)

    wait_all(PARTIAL, "space", part_recv)
    spectra = total(part_recv).astype(bf16)
    u_rows = spectra[0]
    d_wide = spectra[1].astype(f32)
    row = lax.broadcasted_iota(jnp.int32, (16, C), 0)
    even = row % 2 == 0
    d_turned = jnp.where(even, pltpu.roll(d_wide, 15, 0), -pltpu.roll(d_wide, 1, 0))
    scale = jnp.where((row // 2 == 0) & (sp == 0), 1.0, 2.0).astype(f32) / (GRID * GRID)
    d_both = jnp.concatenate([d_wide, d_turned], axis=0).astype(bf16)
    back = jnp.zeros((16, C), f32)
    for k in range(N):
        product = dot(d_both, turned[k])
        back = jnp.where(row // 2 == k, product[0:16, 0:C] + product[16:32, C:], back)
    back_send[...] = (back * scale).astype(bf16)
    send_all(BACK, "space", back_send, back_recv, each=False)

    wait_all(SUM_Z, "z", sumz_recv)
    sumy_send[...] = total(sumz_recv)
    send_all(SUM_YX, "yx", sumy_send, sumy_recv, each=False)

    wait_all(BACK, "space", back_recv)
    grad_send[...] = dot(yb[...], back_recv[...].reshape(2 * MODES, C)).astype(bf16).reshape(MODES, N, C)
    grad_copy = to_all_dp(GRAD, grad_send, grad_recv)

    wait_all(SUM_YX, "yx", sumy_recv)
    sums = total(sumy_recv)
    sumb_send[...] = sums[0:16]
    send_all(SUM_BACK, "space", sumb_send, sumb_recv, each=False)
    out_bias[...] = jnp.sum(sums[16:24], axis=0, keepdims=True)

    d_pair = jnp.concatenate([d_wide, d_turned], axis=1)
    row2 = lax.broadcasted_iota(jnp.int32, (16, 2 * C), 0)
    for k in range(N):
        chosen = jnp.where(row2 // 2 == k, d_pair, 0.0).astype(bf16)
        product = lax.dot_general(
            u_rows, chosen, (((0,), (0,)), ((), ())), preferred_element_type=f32
        )
        scale_k = (jnp.where(sp == 0, 1.0, 2.0) if k == 0 else 2.0) / (GRID * GRID)
        for part in range(2):
            out_spec[0, k, part] = (product[:, part * C : (part + 1) * C] * scale_k).astype(bf16)


    drain()
    grad_copy.wait_recv()
    arrived = grad_recv[...].reshape(GRID, C)
    theirs = dot(xb[pl.ds((1 - core) * COLS * MODES, COLS * MODES), :], arrived)
    swap_rows[...] = theirs.astype(bf16).reshape(COLS, MODES, C)
    rows_copy = to_twin(ROWS, swap_rows, held_rows)
    started.clear()
    mine = dot(xb[pl.ds(core * COLS * MODES, COLS * MODES), :], arrived)
    mine = mine.astype(bf16).astype(f32)
    for t in range(COLS):
        rows_f[pl.ds(core * COLS + t, MODES, stride=N), :] = mine[t * MODES : (t + 1) * MODES]

    wait_all(SUM_BACK, "space", sumb_recv)
    out_local[...] = sumb_recv[...].reshape(C, C)

    rows_copy.wait()
    for t in range(COLS):
        rows_f[pl.ds((1 - core) * COLS + t, MODES, stride=N), :] = held_rows[t].astype(f32)
    out_grad[...] = (rows_f[...] + local_part[...]).reshape(1, MODES, N, C).astype(bf16)


def hand_over(*refs):
    copies = [pltpu.make_async_copy(refs[i], refs[4 + i], refs[-1].at[i]) for i in range(4)]
    for copy in copies:
        copy.start()
    for copy in copies:
        copy.wait()


def on_device(field_in, pre_act, cotangent, spec_weight, local_weight):
    anywhere = pl.BlockSpec(memory_space=pl.ANY)
    in_vmem = pl.BlockSpec(memory_space=pltpu.VMEM)
    block = pltpu.VMEM((MODES, N, C), bf16)
    rows = pltpu.VMEM((GRID, C), f32)
    results = pl.pallas_call(
        kernel,
        out_shape=(
            pltpu.VMEM((1, MODES, N, C), bf16),
            pltpu.VMEM((1, N, 2, C, C), bf16),
            pltpu.VMEM((C, C), f32),
            pltpu.VMEM((1, C), f32),
        ),
        in_specs=[anywhere] * 9,
        out_specs=(in_vmem,) * 4,
        scratch_shapes=[
            block, block, block,
            pltpu.VMEM((N, 2 * C, C), bf16),
            pltpu.VMEM((N, C, 2 * C), bf16),
            pltpu.VMEM((C, C), bf16),
            pltpu.VMEM((2 * MODES, 2 * MODES), bf16),
            pltpu.VMEM((4 * MODES, 2 * GRID), bf16),
            pltpu.VMEM((GRID, 2 * MODES), bf16),
            pltpu.VMEM((GRID, GRID), bf16),
            rows, rows, rows,
            pltpu.VMEM((MODES, COLS * C), bf16),
            pltpu.VMEM((MODES, COLS * C), bf16),
            pltpu.VMEM((2, MODES, COLS * C), bf16),
            pltpu.VMEM((2, MODES, COLS * C), bf16),
            pltpu.VMEM((2 * GRID, C), f32),
            pltpu.VMEM((MODES, 2 * N, C), bf16),
            pltpu.VMEM((MODES, 2 * N, C), bf16),
            pltpu.VMEM((N, 2, 16, C), f32),
            pltpu.VMEM((N, 2, 16, C), f32),
            pltpu.VMEM((16, C), bf16),
            pltpu.VMEM((N, 16, C), bf16),
            block, block,
            pltpu.VMEM((COLS, MODES, C), bf16),
            pltpu.VMEM((COLS, MODES, C), bf16),
            pltpu.VMEM((N, 24, C), f32),
            pltpu.VMEM((N, 24, C), f32),
            pltpu.VMEM((24, C), f32),
            pltpu.VMEM((N, 24, C), f32),
            pltpu.VMEM((24, C), f32),
            pltpu.VMEM((N, 24, C), f32),
            pltpu.VMEM((16, C), f32),
            pltpu.VMEM((N, 16, C), f32),
            pltpu.SemaphoreType.DMA((9,)),
            pltpu.SemaphoreType.DMA((6,)),
            pltpu.SemaphoreType.DMA((6,)),
            pltpu.SemaphoreType.DMA((5,)),
            pltpu.SemaphoreType.DMA((5,)),
            pltpu.SemaphoreType.REGULAR,
        ],
        compiler_params=pltpu.CompilerParams(
            collective_id=0, has_side_effects=True, vmem_limit_bytes=int(62 * 1024 * 1024)
        ),
        cost_estimate=pl.CostEstimate(
            flops=250_000_000, bytes_accessed=2_500_000, transcendentals=65536
        ),
    )(
        field_in, pre_act, cotangent, spec_weight.reshape(N, 2 * C, C), local_weight,
        *(jnp.asarray(t) for t in tables()),
    )
    grad_input, grad_spectral, grad_local, grad_bias = pl.pallas_call(
        hand_over,
        out_shape=tuple(jax.ShapeDtypeStruct(r.shape, r.dtype) for r in results),
        in_specs=[in_vmem] * 4,
        out_specs=(anywhere,) * 4,
        scratch_shapes=[pltpu.SemaphoreType.DMA((4,))],
        compiler_params=pltpu.CompilerParams(vmem_limit_bytes=1024 * 1024),
    )(*results)
    return grad_input, grad_spectral, grad_local, grad_bias.reshape(C)


def solution(mesh):
    placed = (
        P(None, "space", "dp", None),
        P(None, "space", "dp", None),
        P(None, "space", "dp", None),
        P("dp", "space", None, None, None),
        P(),
    )
    return jax.shard_map(
        on_device,
        mesh=mesh,
        in_specs=placed,
        out_specs=(P(None, "space", "dp", None), P("dp", "space", None, None, None), P(), P()),
        check_vma=False,
    )
```

```python
import math

import jax
import jax.numpy as jnp
import numpy as np
from jax import lax
from jax.experimental import pallas as pl
from jax.experimental.pallas import tpu as pltpu
from jax.sharding import PartitionSpec as P

root_two_pi = 0.7978845608028654
cubic_coef = 0.044715

N = 8
C = 128
GRID = 512
MODES = 64
COLS = 4
f32 = jnp.float32
bf16 = jnp.bfloat16

Z_ORDER = [4, 3, 5, 2, 6, 1, 7]
YX_ORDER = [(1, 2), (0, 2), (1, 1), (1, 3), (0, 1), (0, 3), (1, 0)]
SPACE_ORDER = [(2, 0), (2, 1), (1, 0), (3, 0), (1, 1), (3, 1), (0, 1)]
DP_ORDER = sorted(
    [(l, x, z) for l in range(2) for x in range(4) for z in range(8) if l or x or z],
    key=lambda o: -(o[0] + min(o[1], 4 - o[1]) + min(o[2], 8 - o[2])),
)
PARTIAL, BACK, SUM_SPACE, SUM_Z, SUM_YX, SUM_BACK = range(6)
FIELD, DELTA, ROWS, SPEC, GRAD = range(5)


def gelu_slope(values):
    tangent = jnp.tanh(root_two_pi * (values + cubic_coef * values * values * values))
    return 0.5 * (1.0 + tangent) + 0.5 * values * (1.0 - tangent * tangent) * root_two_pi * (
        1.0 + 3.0 * cubic_coef * values * values
    )


def trig(phases):
    angles = (phases % GRID).astype(np.float32) * np.float32(2.0 * math.pi / GRID)
    return np.cos(angles), np.sin(angles)


def tables():
    j = np.arange(MODES)
    frequency = np.where(j < MODES // 2, j, j - MODES)
    c, s = trig(frequency[:, None] * np.arange(GRID)[None, :])
    both = np.stack([c, s]).reshape(2, MODES, 4, 2 * MODES)
    x_table = both.transpose(2, 0, 1, 3).reshape(4, 2 * MODES, 2 * MODES)
    by_row = both.reshape(2, MODES, 4, 2, MODES).transpose(2, 3, 4, 1, 0)
    same = np.eye(COLS)
    x_back = np.einsum("hoxjp,tu->hotxjpu", by_row, same).reshape(4, GRID, GRID)
    y = np.arange(MODES)[None, :, None] * N + np.arange(2)[:, None, None] * COLS + np.arange(COLS)
    c, s = trig(np.arange(MODES)[None, :, None, None] * y[:, None])
    turn = np.stack([np.stack([c, -s], axis=-2), np.stack([-s, -c], axis=-2)], axis=2)
    y_table = turn.reshape(2, 2 * MODES, GRID)
    y_back = turn.transpose(0, 3, 4, 5, 1, 2).reshape(2, GRID, 2 * MODES)
    return [t.astype(bf16) for t in (x_table, y_table, y_back, x_back)]


def dot(a, b):
    return jnp.dot(a, b, preferred_element_type=f32)


def dot_nt(a, b):
    return lax.dot_general(a, b, (((1,), (1,)), ((), ())), preferred_element_type=f32)


def kernel(
    field_hbm, pre_hbm, cot_hbm, weight_hbm, lw_hbm, xt_hbm, yt_hbm, yb_hbm, xb_hbm,
    out_grad, out_spec, out_local, out_bias,
    field_v, pre_v, cot_v, weight, turned, lw, xt, yt, yb, xb,
    rows_f, rows_d, local_part, swap_f, swap_d, held_f, held_d, stage,
    spec_send, spec_recv, part_send, part_recv, back_send, back_recv, grad_send, grad_recv,
    swap_rows, held_rows,
    sum_send, sum_recv, sumz_send, sumz_recv, sumy_send, sumy_recv, sumb_send, sumb_recv,
    in_sem, send_sem, recv_sem, wide_send, wide_recv, lines_in,
):
    sp = lax.axis_index("space")
    dp = lax.axis_index("dp")
    yx = dp // N
    z = dp - yx * N
    row_chip = sp // 2
    core = sp - row_chip * 2
    twin = {"dp": dp, "space": row_chip * 2 + 1 - core}

    def peer(axis, o):
        if axis == "space":
            chip, side = SPACE_ORDER[o - 1]
            other = lax.rem(row_chip + chip, 4) * 2 + lax.rem(core + side, 2)
            return other, sp, {"dp": dp, "space": other}
        if axis == "z":
            other = lax.rem(z + Z_ORDER[o - 1], N)
            return other, z, {"dp": yx * N + other, "space": sp}
        low, x = YX_ORDER[o - 1]
        other = lax.rem(yx // 4 + low, 2) * 4 + lax.rem(yx % 4 + x, 4)
        return other, yx, {"dp": other * N + z, "space": sp}

    def dp_peer(offset):
        low, x, deep = offset
        chips = lax.rem(yx // 4 + low, 2) * 4 + lax.rem(yx % 4 + x, 4)
        return chips * N + lax.rem(z + deep, N)

    loads = []
    for i, (src, dst) in enumerate((
        (field_hbm.at[0], field_v), (pre_hbm.at[0], pre_v), (cot_hbm.at[0], cot_v),
        (xt_hbm.at[row_chip], xt), (lw_hbm, lw), (yt_hbm.at[core], yt),
        (weight_hbm, weight), (yb_hbm.at[core], yb), (xb_hbm.at[row_chip], xb),
    )):
        loads.append(pltpu.make_async_copy(src, dst, in_sem.at[i]))
    for load in loads[:3]:
        load.start()

    barrier = pltpu.get_barrier_semaphore()
    for axis in ("z", "yx", "space"):
        for o in range(1, N):
            pl.semaphore_signal(barrier, inc=1, device_id=peer(axis, o)[2])
    for load in loads[3:]:
        load.start()

    started = []

    def drain():
        while started:
            started.pop(0).wait_send()


    def send_all(hop, axis, src, dst, each=True):
        for o in range(1, N):
            other, me, device = peer(axis, o)
            copy = pltpu.make_async_remote_copy(
                src_ref=src.at[other] if each else src,
                dst_ref=dst.at[me],
                send_sem=send_sem.at[hop],
                recv_sem=recv_sem.at[hop],
                device_id=device,
            )
            copy.start()
        seven = dst.at[pl.ds(0, N - 1)]
        started.append(pltpu.make_async_remote_copy(
            src_ref=seven,
            dst_ref=seven,
            send_sem=send_sem.at[hop],
            recv_sem=recv_sem.at[hop],
            device_id=twin,
        ))
        me = {"space": sp, "z": z, "yx": yx}[axis]
        dst[me] = src[me] if each else src[...]

    def wait_all(hop, axis, dst):
        seven = dst.at[pl.ds(0, N - 1)]
        pltpu.make_async_remote_copy(
            src_ref=seven,
            dst_ref=seven,
            send_sem=send_sem.at[hop],
            recv_sem=recv_sem.at[hop],
            device_id=twin,
        ).wait_recv()

    def to_twin(hop, src, dst):
        copy = pltpu.make_async_remote_copy(
            src_ref=src, dst_ref=dst, send_sem=wide_send.at[hop], recv_sem=wide_recv.at[hop],
            device_id=twin,
        )
        copy.start()
        started.append(copy)
        return copy

    def to_all_dp(hop, src, dst, before_others=None):
        on_lines = lambda o: o[2] == 0 or o[:2] == (0, 0)
        order = DP_ORDER if before_others is None else sorted(DP_ORDER, key=lambda o: not on_lines(o))
        for place, offset in enumerate(order):
            if before_others is not None and place == 2 * (N - 1):
                before_others()
            other = dp_peer(offset)
            pltpu.make_async_remote_copy(
                src_ref=src.at[other],
                dst_ref=dst.at[dp],
                send_sem=wide_send.at[hop],
                recv_sem=wide_recv.at[hop],
                device_id={"dp": other, "space": sp},
            ).start()
        dst[dp] = src[dp]
        whole = pltpu.make_async_remote_copy(
            src_ref=src.at[pl.ds(0, MODES - 1)],
            dst_ref=dst.at[pl.ds(0, MODES - 1)],
            send_sem=wide_send.at[hop],
            recv_sem=wide_recv.at[hop],
            device_id={"dp": lax.rem(dp + 1, MODES), "space": sp},
        )
        started.append(whole)
        return whole

    def total(ref):
        acc = ref[0]
        for i in range(1, N):
            acc = acc + ref[i]
        return acc

    def split(rows, swap):
        for t in range(COLS):
            theirs = rows[pl.ds((1 - core) * COLS + t, MODES, stride=N), :]
            swap[:, t * C : (t + 1) * C] = theirs.astype(bf16)

    def keep(rows, held):
        for t in range(COLS):
            mine = rows[pl.ds(core * COLS + t, MODES, stride=N), :]
            held[core, :, t * C : (t + 1) * C] = mine.astype(bf16)

    loads[0].wait()
    rows_f[...] = field_v[...].astype(f32).reshape(GRID, C)
    split(rows_f, swap_f)
    loads[1].wait()
    loads[2].wait()
    delta = (cot_v[...].astype(f32) * gelu_slope(pre_v[...].astype(f32))).astype(bf16)
    delta_wide = delta.astype(f32)
    rows_d[...] = delta_wide.reshape(GRID, C)
    split(rows_d, swap_d)
    pl.semaphore_wait(barrier, 3 * (N - 1))
    field_copy = to_twin(FIELD, swap_f, held_f.at[core])
    delta_copy = to_twin(DELTA, swap_d, held_d.at[core])
    for o in range(1, N):
        pl.semaphore_signal(lines_in, inc=1, device_id=peer("yx", o)[2])

    keep(rows_f, held_f)
    keep(rows_d, held_d)

    loads[3].wait()

    def transform(held, f):
        product = dot(xt[...], held[...].reshape(2 * MODES, COLS * C))
        for part in range(2):
            for t in range(COLS):
                stage[f, pl.ds(part * COLS + t, MODES, stride=N), :] = product[
                    part * MODES : (part + 1) * MODES, t * C : (t + 1) * C
                ]

    field_copy.wait_recv()
    transform(held_f, 0)
    delta_copy.wait_recv()
    transform(held_d, 1)
    for f in range(2):
        spec_send[:, :, f * C : (f + 1) * C] = stage[f].astype(bf16).reshape(MODES, N, C)
    spec_copy = to_all_dp(
        SPEC, spec_send, spec_recv, lambda: pl.semaphore_wait(lines_in, N - 1)
    )

    field_rows = rows_f[...].astype(bf16)
    delta_rows = rows_d[...].astype(bf16)
    local = lax.dot_general(
        field_rows, delta_rows, (((0,), (0,)), ((), ())), preferred_element_type=f32
    )
    bias_part = jnp.sum(delta_wide, axis=0)
    for t in range(N):
        sum_send[t, 0:16, :] = local[16 * t : 16 * t + 16, :]
        sum_send[t, 16:24, :] = bias_part
    send_all(SUM_SPACE, "space", sum_send, sum_recv)
    for i in range(4, 9):
        loads[i].wait()
    local_part[...] = dot_nt(delta_rows, lw[...])
    for k in range(N):
        turned[k] = weight[k].T

    spec_copy.wait_recv()
    part_send[...] = dot(yt[...], spec_recv[...].reshape(GRID, 2 * C)).reshape(N, 16, 2 * C)
    send_all(PARTIAL, "space", part_send, part_recv)

    wait_all(SUM_SPACE, "space", sum_recv)
    sumz_send[...] = total(sum_recv)
    send_all(SUM_Z, "z", sumz_send, sumz_recv, each=False)

    wait_all(PARTIAL, "space", part_recv)
    spectra = total(part_recv).astype(bf16)
    u_rows = spectra[:, 0:C]
    d_wide = spectra[:, C:].astype(f32)
    row = lax.broadcasted_iota(jnp.int32, (16, C), 0)
    even = row % 2 == 0
    d_turned = jnp.where(even, pltpu.roll(d_wide, 15, 0), -pltpu.roll(d_wide, 1, 0))
    scale = jnp.where((row // 2 == 0) & (sp == 0), 1.0, 2.0).astype(f32) / (GRID * GRID)
    d_both = jnp.concatenate([d_wide, d_turned], axis=0).astype(bf16)
    back = jnp.zeros((16, C), f32)
    for k in range(N):
        product = dot(d_both, turned[k])
        back = jnp.where(row // 2 == k, product[0:16, 0:C] + product[16:32, C:], back)
    back_send[...] = (back * scale).astype(bf16)
    send_all(BACK, "space", back_send, back_recv, each=False)

    wait_all(SUM_Z, "z", sumz_recv)
    sumy_send[...] = total(sumz_recv)
    send_all(SUM_YX, "yx", sumy_send, sumy_recv, each=False)

    wait_all(BACK, "space", back_recv)
    grad_send[...] = dot(yb[...], back_recv[...].reshape(2 * MODES, C)).astype(bf16).reshape(MODES, N, C)
    grad_copy = to_all_dp(GRAD, grad_send, grad_recv)

    wait_all(SUM_YX, "yx", sumy_recv)
    sums = total(sumy_recv)
    sumb_send[...] = sums[0:16]
    send_all(SUM_BACK, "space", sumb_send, sumb_recv, each=False)
    out_bias[...] = jnp.sum(sums[16:24], axis=0, keepdims=True)

    d_pair = jnp.concatenate([d_wide, d_turned], axis=1)
    row2 = lax.broadcasted_iota(jnp.int32, (16, 2 * C), 0)
    for k in range(N):
        chosen = jnp.where(row2 // 2 == k, d_pair, 0.0).astype(bf16)
        product = lax.dot_general(
            u_rows, chosen, (((0,), (0,)), ((), ())), preferred_element_type=f32
        )
        scale_k = (jnp.where(sp == 0, 1.0, 2.0) if k == 0 else 2.0) / (GRID * GRID)
        for part in range(2):
            out_spec[0, k, part] = (product[:, part * C : (part + 1) * C] * scale_k).astype(bf16)


    drain()
    grad_copy.wait_recv()
    arrived = grad_recv[...].reshape(GRID, C)
    theirs = dot(xb[pl.ds((1 - core) * COLS * MODES, COLS * MODES), :], arrived)
    swap_rows[...] = theirs.astype(bf16).reshape(COLS, MODES, C)
    rows_copy = to_twin(ROWS, swap_rows, held_rows)
    started.clear()
    mine = dot(xb[pl.ds(core * COLS * MODES, COLS * MODES), :], arrived)
    mine = mine.astype(bf16).astype(f32)
    for t in range(COLS):
        rows_f[pl.ds(core * COLS + t, MODES, stride=N), :] = mine[t * MODES : (t + 1) * MODES]

    wait_all(SUM_BACK, "space", sumb_recv)
    out_local[...] = sumb_recv[...].reshape(C, C)

    rows_copy.wait()
    for t in range(COLS):
        rows_f[pl.ds((1 - core) * COLS + t, MODES, stride=N), :] = held_rows[t].astype(f32)
    out_grad[...] = (rows_f[...] + local_part[...]).reshape(1, MODES, N, C).astype(bf16)


def hand_over(*refs):
    copies = [pltpu.make_async_copy(refs[i], refs[4 + i], refs[-1].at[i]) for i in range(4)]
    for copy in copies:
        copy.start()
    for copy in copies:
        copy.wait()


def on_device(field_in, pre_act, cotangent, spec_weight, local_weight):
    anywhere = pl.BlockSpec(memory_space=pl.ANY)
    in_vmem = pl.BlockSpec(memory_space=pltpu.VMEM)
    block = pltpu.VMEM((MODES, N, C), bf16)
    rows = pltpu.VMEM((GRID, C), f32)
    results = pl.pallas_call(
        kernel,
        out_shape=(
            pltpu.VMEM((1, MODES, N, C), bf16),
            pltpu.VMEM((1, N, 2, C, C), bf16),
            pltpu.VMEM((C, C), f32),
            pltpu.VMEM((1, C), f32),
        ),
        in_specs=[anywhere] * 9,
        out_specs=(in_vmem,) * 4,
        scratch_shapes=[
            block, block, block,
            pltpu.VMEM((N, 2 * C, C), bf16),
            pltpu.VMEM((N, C, 2 * C), bf16),
            pltpu.VMEM((C, C), bf16),
            pltpu.VMEM((2 * MODES, 2 * MODES), bf16),
            pltpu.VMEM((2 * MODES, GRID), bf16),
            pltpu.VMEM((GRID, 2 * MODES), bf16),
            pltpu.VMEM((GRID, GRID), bf16),
            rows, rows, rows,
            pltpu.VMEM((MODES, COLS * C), bf16),
            pltpu.VMEM((MODES, COLS * C), bf16),
            pltpu.VMEM((2, MODES, COLS * C), bf16),
            pltpu.VMEM((2, MODES, COLS * C), bf16),
            pltpu.VMEM((2, GRID, C), f32),
            pltpu.VMEM((MODES, N, 2 * C), bf16),
            pltpu.VMEM((MODES, N, 2 * C), bf16),
            pltpu.VMEM((N, 16, 2 * C), f32),
            pltpu.VMEM((N, 16, 2 * C), f32),
            pltpu.VMEM((16, C), bf16),
            pltpu.VMEM((N, 16, C), bf16),
            block, block,
            pltpu.VMEM((COLS, MODES, C), bf16),
            pltpu.VMEM((COLS, MODES, C), bf16),
            pltpu.VMEM((N, 24, C), f32),
            pltpu.VMEM((N, 24, C), f32),
            pltpu.VMEM((24, C), f32),
            pltpu.VMEM((N, 24, C), f32),
            pltpu.VMEM((24, C), f32),
            pltpu.VMEM((N, 24, C), f32),
            pltpu.VMEM((16, C), f32),
            pltpu.VMEM((N, 16, C), f32),
            pltpu.SemaphoreType.DMA((9,)),
            pltpu.SemaphoreType.DMA((6,)),
            pltpu.SemaphoreType.DMA((6,)),
            pltpu.SemaphoreType.DMA((5,)),
            pltpu.SemaphoreType.DMA((5,)),
            pltpu.SemaphoreType.REGULAR,
        ],
        compiler_params=pltpu.CompilerParams(
            collective_id=0, has_side_effects=True, vmem_limit_bytes=int(62 * 1024 * 1024)
        ),
        cost_estimate=pl.CostEstimate(
            flops=250_000_000, bytes_accessed=2_500_000, transcendentals=65536
        ),
    )(
        field_in, pre_act, cotangent, spec_weight.reshape(N, 2 * C, C), local_weight,
        *(jnp.asarray(t) for t in tables()),
    )
    grad_input, grad_spectral, grad_local, grad_bias = pl.pallas_call(
        hand_over,
        out_shape=tuple(jax.ShapeDtypeStruct(r.shape, r.dtype) for r in results),
        in_specs=[in_vmem] * 4,
        out_specs=(anywhere,) * 4,
        scratch_shapes=[pltpu.SemaphoreType.DMA((4,))],
        compiler_params=pltpu.CompilerParams(vmem_limit_bytes=1024 * 1024),
    )(*results)
    return grad_input, grad_spectral, grad_local, grad_bias.reshape(C)


def solution(mesh):
    placed = (
        P(None, "space", "dp", None),
        P(None, "space", "dp", None),
        P(None, "space", "dp", None),
        P("dp", "space", None, None, None),
        P(),
    )
    return jax.shard_map(
        on_device,
        mesh=mesh,
        in_specs=placed,
        out_specs=(P(None, "space", "dp", None), P("dp", "space", None, None, None), P(), P()),
        check_vma=False,
    )
```
